512 devices in a mesh: dp: 64 (over y, z), tensor: 8 (over x, core).
Axes of the slice: x: 4, y: 8, z: 8, core: 2. Of those that a mesh axis runs over, the one named last changes fastest.
Arguments:
- normed: bfloat16 [16384, 4608], P(('dp', 'tensor')), may hold values from -32 to 32
- seg_ids: int32 [64, 256], P('dp'), may hold values from 0 to 3, never falling along the last dimension, each value on 1 to 128 neighbouring positions
- w_query: bfloat16 [4608, 2048], P('dp', 'tensor'), may hold values from -0.09375 to 0.09375
- w_key: bfloat16 [4608, 1024], P('dp', 'tensor'), may hold values from -0.09375 to 0.09375
- w_value: bfloat16 [4608, 1024], P('dp', 'tensor'), may hold values from -0.09375 to 0.09375
- grad_attn: bfloat16 [16384, 2048], P('dp', 'tensor'), may hold values from -6 to 6
Outputs:
- input_grad: bfloat16 [16384, 4608], P(('dp', 'tensor'))
- value_weight_grad: float32 [4608, 1024], P('dp', 'tensor')
The draws below stay inside these ranges and needn't reach their ends.
All inputs are finite; a program needn't handle non-finite values.
Results may differ from the reference program's by a relative error of at most 0.019.
Values may be sent and summed in bfloat16 or wider, within the bound.
A program may use at most 64 MiB of HBM per device.

```python
import math
import jax
import jax.numpy as jnp
import numpy as np
from jax import lax

D = 4608
HD = 128
GROUP = 2
TOK_DEV = 256
KVH = 8
QH = 16
GROUPS = 64
TOKENS = 16384


def draw_normed(key, part):
    key = jax.random.fold_in(key, 11)
    base_key, scale_key = jax.random.split(key)
    base = jnp.clip(jax.random.normal(base_key, (TOKENS, D), jnp.float32), -4.0, 4.0)
    scales = jnp.exp(jax.random.uniform(scale_key, (TOKENS, 1), jnp.float32, math.log(0.3), math.log(3.0)))
    return (base * scales).astype(jnp.bfloat16)


def block_levels(key, dims, pieces, low, high):
    factor_of = 1.0
    for position, blocks in pieces:
        heights = jax.random.uniform(jax.random.fold_in(jax.random.fold_in(key, 6), position), (blocks,), jnp.float32, low / len(pieces), high / len(pieces))
        factor_of = factor_of * jnp.repeat(jnp.exp(heights), dims[position] // blocks).reshape((-1,) + (1,) * (len(dims) - 1 - position))
    return factor_of


def split_up(amount, total, bound, skew):
    loads = [(1 << 20) // math.isqrt(standing ** skew) + 1 for standing in range(2, amount + 1)]
    surplus, holding = total - bound - (amount - 1), [1] * (amount - 1)
    while surplus > 0:
        candidates = [i for i in range(amount - 1) if holding[i] < bound]
        whole, budget = sum([loads[i] for i in candidates]), surplus
        for i in candidates:
            more = min(bound - holding[i], max(1, budget * loads[i] // whole), surplus)
            holding[i] = holding[i] + more
            surplus = surplus - more
    return np.array([bound] + holding)


def ragged(stream_key, count, total, reach, lean):
    if count == 2:
        one = jax.random.randint(stream_key, (), max(1, total - reach), min(reach, total - 1) + 1)
        return jnp.stack([one, total - one])
    sizes = jnp.asarray(split_up(count, total, reach, lean), jnp.int32)
    couples = (count - 1) // 2
    donor, sink = sizes[1:1 + 2 * couples:2], sizes[2:2 + 2 * couples:2]
    margin = jnp.minimum(donor - 1, reach - sink)
    shifted = jax.random.randint(jax.random.fold_in(stream_key, 1), (couples,), 0, 1 << 20) % (margin + 1)
    sizes = sizes.at[1:1 + 2 * couples:2].set(donor - shifted).at[2:2 + 2 * couples:2].set(sink + shifted)
    return sizes[jax.random.permutation(jax.random.fold_in(stream_key, 2), count)]


def normal_values(stream_key, shape, spread, reach, cuts=(), kind=jnp.bfloat16):
    result = spread * jax.random.normal(stream_key, shape, jnp.float32)
    if cuts:
        result = result * block_levels(stream_key, shape, cuts, -0.22, 0.18)
    return jnp.clip(result, -reach, reach).astype(kind)


def setup_inputs(seed: int = 0) -> dict:
    splits = jax.random.split(jax.random.key(seed), 7)
    normed = draw_normed(jax.random.fold_in(splits[6], 71), 0)
    seg_ids = jax.vmap(lambda own: jnp.searchsorted(jnp.cumsum(ragged(own, 4, TOK_DEV, TOK_DEV // 2, 0)), jnp.arange(TOK_DEV), side="right"))(jax.random.split(splits[1], GROUPS)).reshape((GROUPS, TOK_DEV)).astype(jnp.int32)
    w_query = normal_values(splits[2], (D, QH * HD), D ** -0.5, 0.09375, ((0, 64), (1, 8)))
    w_key = normal_values(splits[3], (D, KVH * HD), D ** -0.5, 0.09375, ((0, 64), (1, 8)))
    w_value = normal_values(splits[4], (D, KVH * HD), D ** -0.5, 0.09375, ((0, 64), (1, 8)))
    grad_attn = normal_values(splits[5], (TOKENS, QH * HD), 1.0, 6.0, ((0, 64), (1, 8)))
    return {"normed": normed, "seg_ids": seg_ids, "w_query": w_query, "w_key": w_key, "w_value": w_value, "grad_attn": grad_attn}


query_scale = 1.0 / 12.0
masked_value = -1.0e30


def group_grads(query, key, value, grad, seg, wcat):
    qf = query.astype(jnp.float32)
    kf = key.astype(jnp.float32)
    vf = value.astype(jnp.float32)
    gf = grad.astype(jnp.float32)
    count = seg.shape[0]
    places = jnp.arange(count)
    allowed = (places[None, :] <= places[:, None]) & (seg[:, None] == seg[None, :])
    scores = jnp.einsum('ikgd,jkd->kgij', qf, kf) * query_scale
    scores = jnp.where(allowed, scores, masked_value)
    top = jnp.max(scores, axis=-1, keepdims=True)
    expo = jnp.exp(scores - top)
    probs = expo / jnp.sum(expo, axis=-1, keepdims=True)
    probs_b = probs.astype(jnp.bfloat16).astype(jnp.float32)
    outputs = jnp.einsum('kgij,jkd->ikgd', probs_b, vf)
    delta = jnp.sum(gf * outputs, axis=-1)
    dprobs = jnp.einsum('ikgd,jkd->kgij', gf, vf)
    dscores = (probs * (dprobs - jnp.transpose(delta, (1, 2, 0))[..., None]) * query_scale).astype(jnp.bfloat16)
    dfloat = dscores.astype(jnp.float32)
    grad_query = jnp.einsum('kgij,jkd->ikgd', dfloat, kf).astype(jnp.bfloat16)
    grad_key = jnp.einsum('kgij,ikgd->jkd', dfloat, qf).astype(jnp.bfloat16)
    grad_value = jnp.einsum('kgij,ikgd->jkd', probs_b, gf).astype(jnp.bfloat16)
    heads = grad_query.shape[1]
    gcat = jnp.concatenate([grad_query.reshape(count, heads, -1), grad_key, grad_value], axis=2)
    parts = jnp.einsum('tkc,kcd->ktd', gcat.astype(jnp.float32), wcat)
    parts = parts.astype(jnp.bfloat16).astype(jnp.float32)
    input_rows = jnp.sum(parts, axis=0).astype(jnp.bfloat16)
    return input_rows, grad_value


def reference(normed, seg_ids, w_query, w_key, w_value, grad_attn):
    query = jnp.dot(normed, w_query, preferred_element_type=jnp.float32).astype(jnp.bfloat16)
    key = jnp.dot(normed, w_key, preferred_element_type=jnp.float32).astype(jnp.bfloat16)
    value = jnp.dot(normed, w_value, preferred_element_type=jnp.float32).astype(jnp.bfloat16)
    query = query.reshape(GROUPS, TOK_DEV, KVH, GROUP, HD)
    key = key.reshape(GROUPS, TOK_DEV, KVH, HD)
    value = value.reshape(GROUPS, TOK_DEV, KVH, HD)
    grad = grad_attn.reshape(GROUPS, TOK_DEV, KVH, GROUP, HD)
    wcat = jnp.concatenate([w_query.reshape(D, KVH, GROUP * HD), w_key.reshape(D, KVH, HD), w_value.reshape(D, KVH, HD)], axis=2)
    wcat = jnp.transpose(wcat, (1, 2, 0)).astype(jnp.float32)

    def one_group(items):
        return group_grads(items[0], items[1], items[2], items[3], items[4], wcat)

    input_rows, grad_value = lax.map(one_group, (query, key, value, grad, seg_ids))
    input_grad = input_rows.reshape(TOKENS, D)
    grad_value = grad_value.reshape(TOKENS, KVH * HD)
    value_weight_grad = jnp.dot(normed.T, grad_value, preferred_element_type=jnp.float32) * (float(TOKENS) ** -0.5)
    return input_grad, value_weight_grad
```

```python
import jax
import jax.numpy as jnp
from jax import lax
from jax.experimental import pallas as pl
from jax.experimental.pallas import tpu as pltpu
from jax.sharding import PartitionSpec as P

MESH = pl.DeviceIdType.MESH
F32 = jnp.float32
BF16 = jnp.bfloat16

D = 4608
HD = 128
TOK = 256
RING = 8
XS = 4
ROWS = 72
PAIR = 2 * ROWS
UNIT = RING * ROWS
HALF = D // 2
CHUNK = 2 * UNIT
CHUNKS = D // CHUNK
OWN = 32
LOW, HIGH, HIGH_PAD = 32, 40, 48
QUERY_SCALE = 1.0 / 12.0
MASKED = -1e30
RIGHT, LEFT = 0, 1
SIGN = (1, -1)

NT = (((1,), (1,)), ((), ()))


def dot(a, b):
    return jnp.dot(a, b, preferred_element_type=F32)


def dot_nt(a, b):
    return lax.dot_general(a, b, NT, preferred_element_type=F32)


def kernel(
    normed, seg, w_query, w_key, w_value, grad,
    input_grad, value_grad,
    x_buf, x_t, w_buf, pair_out, pair_in, mask, q_acc, kv_acc, g_cat,
    vw, a_send, a_recv, b_send, b_recv, a_sum, b_sum, a_low, b_high, a_got, b_got,
    part, sib, far_send, far_recv, near_send, near_recv,
    pair_s, pair_r, x_s, x_r, a1_s, a1_r, b1_s, b1_r, a2f_s, b2f_s, a2_s, b2_s, a2_r, b2_r,
    va_s, va_r, vb_s, vb_r, vd_s, vd_r, sib_s, sib_r, far_s, far_r, near_s, near_r,
):
    dp, tensor = lax.axis_index("dp"), lax.axis_index("tensor")
    y, z, x, core = dp // RING, dp % RING, tensor // 2, tensor % 2
    par, m = z % 2, z // 2
    other = 1 - core

    def at(xx, yy, zz, cc):
        return (yy * RING + zz, xx * 2 + cc)

    def shift(position, by, size=RING):
        return (position + by + size) % size

    def y_dev(by):
        return at(x, shift(y, by), z, core)

    def z_dev(by):
        return at(x, y, shift(z, by), core)

    def x_dev(by):
        return at(shift(x, by, XS), y, z, core)

    sibling = at(x, y, z, other)
    partner = at(x, y, z + 1 - 2 * par, core)
    sent = []

    def copy(src, dst, send_sem, recv_sem, device):
        return pltpu.make_async_remote_copy(
            src_ref=src, dst_ref=dst, send_sem=send_sem, recv_sem=recv_sem, device_id=device, device_id_type=MESH
        )

    def send(src, dst, send_sem, recv_sem, device):
        one = copy(src, dst, send_sem, recv_sem, device)
        one.start()
        sent.append(one)

    def arrived(dst, send_sem, recv_sem):
        copy(dst, dst, send_sem, recv_sem, sibling).wait_recv()

    def drain(count):
        for _ in range(count):
            sent.pop(0).wait_send()

    barrier = pltpu.get_barrier_semaphore()
    friends = [sibling, x_dev(1), x_dev(-1)]
    friends += [y_dev(by) for by in range(1, RING)] + [z_dev(by) for by in range(1, RING)]
    for friend in friends:
        pl.semaphore_signal(barrier, inc=1, device_id=friend, device_id_type=MESH)

    q_first, q_second = w_query[:, :HD].astype(F32), w_query[:, HD:].astype(F32)
    k_own, v_own = w_key[...].astype(F32), w_value[...].astype(F32)
    even = par == 0
    keep_q, give_q = jnp.where(even, q_first, q_second), jnp.where(even, q_second, q_first)
    keep_kv, give_kv = jnp.where(even, k_own, v_own), jnp.where(even, v_own, k_own)
    pair_out[...] = jnp.concatenate([give_q, give_kv], axis=0).astype(BF16)

    pl.semaphore_wait(barrier, len(friends))
    send(pair_out, pair_in, pair_s, pair_r, partner)

    def rows_of(xx, cc):
        return pl.ds(pl.multiple_of((2 * xx + cc) * OWN, OWN), OWN)

    here = x_buf.at[rows_of(x, core)]
    send(normed, here, x_s.at[0], x_r.at[0], x_dev(1))
    send(normed, here, x_s.at[1], x_r.at[1], x_dev(-1))
    send(normed, here, x_s.at[2], x_r.at[2], sibling)
    x_buf[rows_of(x, core), :] = normed[...]

    seg_f = seg[...].astype(F32)
    seg_col = jnp.transpose(jnp.broadcast_to(seg_f, (HD, TOK)))
    seg_col = jnp.concatenate([seg_col, seg_col], axis=1)
    key_at = lax.broadcasted_iota(jnp.int32, (TOK, TOK), 0)
    query_at = lax.broadcasted_iota(jnp.int32, (TOK, TOK), 1)
    mask[...] = jnp.where((key_at <= query_at) & (seg_col == seg_f), 1.0, 0.0).astype(F32)

    def unit_a(zz):
        return w_buf.at[zz % 2, y, pl.ds(pl.multiple_of((zz // 2) * PAIR, 16), PAIR)]

    def unit_b(yy):
        return w_buf.at[2 + par, yy, pl.ds(pl.multiple_of(m * PAIR, 16), PAIR)]

    def piece_a(yy, k):
        return w_buf.at[k, yy]

    def piece_b(zz, k):
        return w_buf.at[2 + zz % 2, pl.ds(4 * k, 4), pl.ds(pl.multiple_of((zz // 2) * PAIR, 16), PAIR)]

    arrived(pair_in, pair_s, pair_r)
    got = pair_in[...].astype(F32)
    got_q, got_kv = got[:ROWS], got[ROWS:]
    own_rows = pl.ds(pl.multiple_of(m * PAIR, 16), PAIR)
    w_buf[par, y, own_rows, :] = jnp.where(
        even, jnp.concatenate([keep_q, got_q], axis=0), jnp.concatenate([got_q, keep_q], axis=0)
    ).astype(BF16)
    w_buf[2 + par, y, own_rows, :] = jnp.where(
        even, jnp.concatenate([keep_kv, got_kv], axis=0), jnp.concatenate([got_kv, keep_kv], axis=0)
    ).astype(BF16)

    def first_hop(way, hop):
        by = SIGN[way]
        zz, yy = shift(z, -by * (hop - 1)), shift(y, -by * (hop - 1))
        send(unit_a(zz), unit_a(zz), a1_s.at[way, hop - 1], a1_r.at[way, hop - 1], z_dev(by))
        send(unit_b(yy), unit_b(yy), b1_s.at[way, hop - 1], b1_r.at[way, hop - 1], y_dev(by))

    def turn(zz, yy, index):
        for way in (RIGHT, LEFT):
            by = SIGN[way]
            send(unit_a(zz), unit_a(zz), a2f_s.at[way, index], a2_r.at[way, 0, zz % 2], y_dev(by))
            send(unit_b(yy), unit_b(yy), b2f_s.at[way, index], b2_r.at[way, 0, yy // 4], z_dev(by))

    first_hop(RIGHT, 1)
    first_hop(LEFT, 1)
    turn(z, y, 0)
    index = 0
    for hop in range(1, 5):
        for way in (RIGHT, LEFT):
            if way == LEFT and hop == 4:
                continue
            by = SIGN[way]
            zz, yy = shift(z, -by * hop), shift(y, -by * hop)
            arrived(unit_a(zz), a1_s.at[way, hop - 1], a1_r.at[way, hop - 1])
            arrived(unit_b(yy), b1_s.at[way, hop - 1], b1_r.at[way, hop - 1])
            if hop + 1 <= (4 if way == RIGHT else 3):
                first_hop(way, hop + 1)
            index += 1
            turn(zz, yy, index)

    left_half, right_half = pl.ds(0, HALF), pl.ds(HALF, HALF)
    x_right, x_left, x_far = shift(x, 1, XS), shift(x, -1, XS), shift(x, 2, XS)

    def x_ref(xx, cc, columns=None):
        return x_buf.at[rows_of(xx, cc)] if columns is None else x_buf.at[rows_of(xx, cc), columns]

    def x_forward():
        arrived(x_ref(x_left, core), x_s.at[0], x_r.at[0])
        send(x_ref(x_left, core, left_half), x_ref(x_left, core, left_half), x_s.at[3], x_r.at[3], x_dev(1))
        send(x_ref(x_left, core), x_ref(x_left, core), x_s.at[4], x_r.at[4], sibling)
        arrived(x_ref(x_right, core), x_s.at[1], x_r.at[1])
        send(x_ref(x_right, core, right_half), x_ref(x_right, core, right_half), x_s.at[5], x_r.at[5], x_dev(-1))
        send(x_ref(x_right, core), x_ref(x_right, core), x_s.at[6], x_r.at[6], sibling)

    def x_finish():
        arrived(x_ref(x_far, core, left_half), x_s.at[3], x_r.at[3])
        send(x_ref(x_far, core, left_half), x_ref(x_far, core, left_half), x_s.at[7], x_r.at[7], sibling)
        arrived(x_ref(x_far, core, right_half), x_s.at[5], x_r.at[5])
        send(x_ref(x_far, core, right_half), x_ref(x_far, core, right_half), x_s.at[8], x_r.at[8], sibling)
        arrived(x_ref(x, other), x_s.at[2], x_r.at[2])
        arrived(x_ref(x_left, other), x_s.at[4], x_r.at[4])
        arrived(x_ref(x_right, other), x_s.at[6], x_r.at[6])
        arrived(x_ref(x_far, other, left_half), x_s.at[7], x_r.at[7])
        arrived(x_ref(x_far, other, right_half), x_s.at[8], x_r.at[8])

    def pass_on(hop):
        for k in range(2):
            for way in (RIGHT, LEFT):
                by = SIGN[way]
                yy, zz = shift(y, -by * hop), shift(z, -by * hop)
                if hop == 4 and k != way:
                    continue
                arrived(piece_a(yy, k), a2_s.at[way, 0, k], a2_r.at[way, hop - 1, k])
                if hop < 3 or (hop == 3 and k == way):
                    send(piece_a(yy, k), piece_a(yy, k), a2_s.at[way, hop - 1, k], a2_r.at[way, hop, k], y_dev(by))
                arrived(piece_b(zz, k), b2_s.at[way, 0, k], b2_r.at[way, hop - 1, k])
                if hop < 3 or (hop == 3 and k == way):
                    send(piece_b(zz, k), piece_b(zz, k), b2_s.at[way, hop - 1, k], b2_r.at[way, hop, k], z_dev(by))

    def x_columns(p):
        return x_buf[:, pl.ds(pl.multiple_of(p * CHUNK, HD), CHUNK)]

    def weights(kinds, p):
        return jnp.concatenate([w_buf[kind, pl.ds(2 * p, 2)].reshape(CHUNK, HD) for kind in kinds], axis=1)

    p_own = y // 2
    p_step = 1 - 2 * ((y + 1) % 2)

    x_forward()
    older = len(sent)
    pass_on(1)
    x_finish()
    drain(older)
    older = len(sent)
    q_acc[...] = dot(x_columns(p_own), weights((0, 1), p_own))

    pass_on(2)
    p_next = shift(p_own, p_step, CHUNKS)
    q_acc[...] += dot(x_columns(p_next), weights((0, 1), p_next))

    def flip(i, carry):
        columns = pl.ds(pl.multiple_of(i * 4 * HD, 4 * HD), 4 * HD)
        x_t[columns, :] = jnp.transpose(x_buf[:, columns])
        return carry

    lax.fori_loop(0, D // (4 * HD), flip, 0)
    drain(older)
    older = len(sent)

    pass_on(3)
    p_next = shift(p_own, -p_step, CHUNKS)
    q_acc[...] += dot(x_columns(p_next), weights((0, 1), p_next))
    drain(older)
    pass_on(4)
    p_next = shift(p_own, 2, CHUNKS)
    query = (q_acc[...] + dot(x_columns(p_next), weights((0, 1), p_next))).astype(BF16)

    kv_acc[...] = jnp.zeros_like(kv_acc)

    def project(p, carry):
        kv_acc[...] += dot(x_columns(p), weights((2, 3), p))
        return carry

    lax.fori_loop(0, CHUNKS, project, 0)
    key, value = kv_acc[:, :HD].astype(BF16), kv_acc[:, HD:].astype(BF16)

    allowed = mask[...] > 0.5
    probs, dprobs = [], []
    for h in range(2):
        scores = jnp.where(allowed, dot_nt(key, query[:, h * HD : (h + 1) * HD]) * QUERY_SCALE, MASKED)
        expo = jnp.exp(scores - jnp.max(scores, axis=0, keepdims=True))
        probs.append(expo * (1.0 / jnp.sum(expo, axis=0, keepdims=True)))
        dprobs.append(dot_nt(value, grad[:, h * HD : (h + 1) * HD]))
    rounded = [one.astype(BF16) for one in probs]
    grad_v = (dot(rounded[0], grad[:, :HD]) + dot(rounded[1], grad[:, HD:])).astype(BF16)

    for yy in range(RING):
        vw[yy] = dot(x_t[yy * UNIT : (yy + 1) * UNIT, :], grad_v).reshape(RING, ROWS, HD)

    def vw_low(yy, k):
        return vw[yy, 4 * k : 4 * k + 4, :LOW, :]

    def vw_high(zz, k):
        return vw[4 * k : 4 * k + 4, zz, LOW:, :]

    def pad(block):
        return jnp.concatenate([block, jnp.zeros((4, HIGH_PAD - HIGH, HD), F32)], axis=1)

    def vw_step(step, k, way):
        by = SIGN[way]
        low, high = vw_low(shift(y, by * (5 - step)), k), vw_high(shift(z, by * (5 - step)), k)
        if step > 2 or (step == 2 and k == way):
            arrived(a_recv.at[way, step - 2, k], va_s.at[way, step - 2, k], va_r.at[way, step - 2, k])
            arrived(b_recv.at[way, step - 2, k], vb_s.at[way, step - 2, k], vb_r.at[way, step - 2, k])
            low = low + a_recv[way, step - 2, k].astype(F32)
            high = high + b_recv[way, step - 2, k][:, :HIGH, :].astype(F32)
        a_send[way, step - 1, k] = low.astype(BF16)
        b_send[way, step - 1, k] = pad(high).astype(BF16)
        slot = (way, step - 1, k)
        send(a_send.at[slot], a_recv.at[slot], va_s.at[slot], va_r.at[slot], y_dev(by))
        send(b_send.at[slot], b_recv.at[slot], vb_s.at[slot], vb_r.at[slot], z_dev(by))

    def vw_turn():
        for k in range(2):
            low, high = vw_low(y, k), vw_high(z, k)
            for way in (RIGHT, LEFT):
                slot = (way, 3, k)
                arrived(a_recv.at[slot], va_s.at[slot], va_r.at[slot])
                arrived(b_recv.at[slot], vb_s.at[slot], vb_r.at[slot])
                low = low + a_recv[slot].astype(F32)
                high = high + b_recv[slot][:, :HIGH, :].astype(F32)
            a_sum[4 * k : 4 * k + 4] = low
            b_sum[4 * k : 4 * k + 4] = high
            a_low[4 * k : 4 * k + 4] = low.astype(BF16)
            b_high[4 * k : 4 * k + 4] = pad(high).astype(BF16)
        for by in range(1, RING):
            zz, yy = shift(z, by), shift(y, by)
            send(a_low.at[zz], a_got.at[by - 1], vd_s.at[0, by - 1], vd_r.at[0, by - 1], z_dev(by))
            send(b_high.at[yy], b_got.at[by - 1], vd_s.at[1, by - 1], vd_r.at[1, by - 1], y_dev(by))

    def vw_finish():
        low, high = a_sum[z], b_sum[y]
        for by in range(1, RING):
            arrived(a_got.at[by - 1], vd_s.at[0, by - 1], vd_r.at[0, by - 1])
            arrived(b_got.at[by - 1], vd_s.at[1, by - 1], vd_r.at[1, by - 1])
            low = low + a_got[by - 1].astype(F32)
            high = high + b_got[by - 1][:HIGH].astype(F32)
        scale = float(TOK * RING * RING) ** (-0.5)
        value_grad[:LOW, :] = low * scale
        value_grad[LOW:, :] = high * scale

    for way in (RIGHT, LEFT):
        vw_step(1, way, way)
    for way in (RIGHT, LEFT):
        vw_step(2, 1 - way, way)

    dscores = []
    for h in range(2):
        delta = jnp.sum(rounded[h].astype(F32) * dprobs[h], axis=0, keepdims=True)
        dscores.append((probs[h] * (dprobs[h] - delta) * QUERY_SCALE).astype(BF16))
    key_t = jnp.transpose(key)
    for h in range(2):
        g_cat[:, h * HD : (h + 1) * HD] = jnp.transpose(dot(key_t, dscores[h])).astype(BF16)
    g_cat[:, 2 * HD : 3 * HD] = (dot(dscores[0], query[:, :HD]) + dot(dscores[1], query[:, HD:])).astype(BF16)
    g_cat[:, 3 * HD :] = grad_v

    def ig_part(q):
        both = dot_nt(g_cat[...], weights((0, 1, 2, 3), q)).astype(BF16)
        part[q] = both.reshape(XS, 2, OWN, CHUNK)
        send(part.at[q, :, other], sib.at[q], sib_s.at[q], sib_r.at[q], sibling)

    def chip_sum(q, xx):
        return part[q, xx, core].astype(F32) + sib[q, xx].astype(F32)

    def ig_first(q):
        way = q % 2
        by = SIGN[way]
        arrived(sib.at[q], sib_s.at[q], sib_r.at[q])
        far_send[q] = chip_sum(q, x_far).astype(BF16)
        send(far_send.at[q], far_recv.at[q], far_s.at[q], far_r.at[q], x_dev(by))
        near_send[q, 1 - way] = chip_sum(q, shift(x, -by, XS)).astype(BF16)
        slot = (q, 1 - way)
        send(near_send.at[slot], near_recv.at[slot], near_s.at[slot], near_r.at[slot], x_dev(-by))

    def ig_second(q):
        way = q % 2
        by = SIGN[way]
        arrived(far_recv.at[q], far_s.at[q], far_r.at[q])
        near_send[q, way] = (chip_sum(q, shift(x, by, XS)) + far_recv[q].astype(F32)).astype(BF16)
        slot = (q, way)
        send(near_send.at[slot], near_recv.at[slot], near_s.at[slot], near_r.at[slot], x_dev(by))

    def ig_finish(q):
        total = chip_sum(q, x)
        for way in (RIGHT, LEFT):
            slot = (q, way)
            arrived(near_recv.at[slot], near_s.at[slot], near_r.at[slot])
            total = total + near_recv[slot].astype(F32)
        input_grad[:, q * CHUNK : (q + 1) * CHUNK] = total.astype(BF16)

    ig_part(0)
    ig_part(1)
    ig_first(0)
    for way in (RIGHT, LEFT):
        vw_step(2, way, way)
    ig_part(2)
    ig_first(1)
    ig_part(3)
    ig_first(2)
    ig_first(3)
    for k in range(2):
        for way in (RIGHT, LEFT):
            vw_step(3, k, way)
    ig_second(0)
    ig_second(1)
    for k in range(2):
        for way in (RIGHT, LEFT):
            vw_step(4, k, way)
    ig_second(2)
    ig_second(3)
    older = len(sent)
    vw_turn()
    drain(older)
    ig_finish(0)
    ig_finish(1)
    vw_finish()
    ig_finish(2)
    ig_finish(3)
    drain(len(sent))


def shards(normed, seg_ids, w_query, w_key, w_value, grad_attn):
    vmem = pl.BlockSpec(memory_space=pltpu.VMEM)
    dma = pltpu.SemaphoreType.DMA
    scratch = [
        pltpu.VMEM((TOK, D), BF16),
        pltpu.VMEM((D, TOK), BF16),
        pltpu.VMEM((4, RING, UNIT, HD), BF16),
        pltpu.VMEM((PAIR, HD), BF16),
        pltpu.VMEM((PAIR, HD), BF16),
        pltpu.VMEM((TOK, TOK), F32),
        pltpu.VMEM((TOK, 2 * HD), F32),
        pltpu.VMEM((TOK, 2 * HD), F32),
        pltpu.VMEM((TOK, 4 * HD), BF16),
        pltpu.VMEM((RING, RING, ROWS, HD), F32),
        pltpu.VMEM((2, 4, 2, 4, LOW, HD), BF16),
        pltpu.VMEM((2, 4, 2, 4, LOW, HD), BF16),
        pltpu.VMEM((2, 4, 2, 4, HIGH_PAD, HD), BF16),
        pltpu.VMEM((2, 4, 2, 4, HIGH_PAD, HD), BF16),
        pltpu.VMEM((RING, LOW, HD), F32),
        pltpu.VMEM((RING, HIGH, HD), F32),
        pltpu.VMEM((RING, LOW, HD), BF16),
        pltpu.VMEM((RING, HIGH_PAD, HD), BF16),
        pltpu.VMEM((RING - 1, LOW, HD), BF16),
        pltpu.VMEM((RING - 1, HIGH_PAD, HD), BF16),
        pltpu.VMEM((CHUNKS, XS, 2, OWN, CHUNK), BF16),
        pltpu.VMEM((CHUNKS, XS, OWN, CHUNK), BF16),
        pltpu.VMEM((CHUNKS, OWN, CHUNK), BF16),
        pltpu.VMEM((CHUNKS, OWN, CHUNK), BF16),
        pltpu.VMEM((CHUNKS, 2, OWN, CHUNK), BF16),
        pltpu.VMEM((CHUNKS, 2, OWN, CHUNK), BF16),
        dma(()), dma(()),
        dma((9,)), dma((9,)),
        dma((2, 4)), dma((2, 4)),
        dma((2, 4)), dma((2, 4)),
        dma((2, RING)), dma((2, RING)),
        dma((2, 3, 2)), dma((2, 3, 2)),
        dma((2, 4, 2)), dma((2, 4, 2)),
        dma((2, 4, 2)), dma((2, 4, 2)),
        dma((2, 4, 2)), dma((2, 4, 2)),
        dma((2, RING - 1)), dma((2, RING - 1)),
        dma((CHUNKS,)), dma((CHUNKS,)),
        dma((CHUNKS,)), dma((CHUNKS,)),
        dma((CHUNKS, 2)), dma((CHUNKS, 2)),
    ]
    return pl.pallas_call(
        kernel,
        out_shape=(jax.ShapeDtypeStruct((OWN, D), BF16), jax.ShapeDtypeStruct((ROWS, HD), F32)),
        in_specs=[vmem] * 6,
        out_specs=(vmem, vmem),
        scratch_shapes=scratch,
        compiler_params=pltpu.CompilerParams(
            collective_id=0, has_side_effects=True, vmem_limit_bytes=50 * 1024 * 1024
        ),
        name="attention_backward",
    )(normed, seg_ids, w_query, w_key, w_value, grad_attn)


def solution(mesh):
    return jax.shard_map(
        shards,
        mesh=mesh,
        in_specs=(
            P(("dp", "tensor"), None),
            P("dp", None),
            P("dp", "tensor"),
            P("dp", "tensor"),
            P("dp", "tensor"),
            P("dp", "tensor"),
        ),
        out_specs=(P(("dp", "tensor"), None), P("dp", "tensor")),
        check_vma=False,
    )
```

```python
import jax
import jax.numpy as jnp
from jax import lax
from jax.experimental import pallas as pl
from jax.experimental.pallas import tpu as pltpu
from jax.sharding import PartitionSpec as P

MESH = pl.DeviceIdType.MESH
F32 = jnp.float32
BF16 = jnp.bfloat16

D = 4608
HD = 128
TOK = 256
RING = 8
XS = 4
ROWS = 72
PAIR = 2 * ROWS
UNIT = RING * ROWS
HALF = D // 2
CHUNK = 2 * UNIT
CHUNKS = D // CHUNK
OWN = 32
PADDED = 80
ENTRIES = (0, -1, 1, -2, 2, -3, 3, -4)
GROUP = 4
QUERY_SCALE = 1.0 / 12.0
MASKED = -1e30
RIGHT, LEFT = 0, 1
SIGN = (1, -1)

NT = (((1,), (1,)), ((), ()))


def dot(a, b):
    return jnp.dot(a, b, preferred_element_type=F32)


def dot_nt(a, b):
    return lax.dot_general(a, b, NT, preferred_element_type=F32)


def kernel(
    normed, seg_hbm, w_query_hbm, w_key_hbm, w_value_hbm, grad_hbm,
    input_grad, value_grad,
    seg, w_query, w_key, w_value, grad,
    x_buf, x_t, x_p, w_buf, pair_out, pair_in, mask, q_acc, kv_acc, g_cat,
    vw, a_send, a_recv, b_send, b_recv, line_sum, line_send, line_recv,
    part, sib, far_send, far_recv, near_send, near_recv,
    in_sem, pair_s, pair_r, x_s, x_r, turn_s, turn_r, pass_s, a_r, b_r,
    v_s, va_r, vb_r, line_s, line_r, sib_s, sib_r, far_s, far_r, near_s, near_r,
):
    dp, tensor = lax.axis_index("dp"), lax.axis_index("tensor")
    y, z, x, core = dp // RING, dp % RING, tensor // 2, tensor % 2
    par, m = z % 2, z // 2
    other = 1 - core

    def at(xx, yy, zz, cc):
        return (yy * RING + zz, xx * 2 + cc)

    def shift(position, by, size=RING):
        return (position + by + size) % size

    def y_dev(by):
        return at(x, shift(y, by), z, core)

    def z_dev(by):
        return at(x, y, shift(z, by), core)

    def x_dev(by):
        return at(shift(x, by, XS), y, z, core)

    sibling = at(x, y, z, other)
    partner = at(x, y, z + 1 - 2 * par, core)

    def copy(src, dst, send_sem, recv_sem, device):
        return pltpu.make_async_remote_copy(
            src_ref=src, dst_ref=dst, send_sem=send_sem, recv_sem=recv_sem, device_id=device, device_id_type=MESH
        )

    def send(src, dst, send_sem, recv_sem, device):
        copy(src, dst, send_sem, recv_sem, device).start()

    def arrived(like, recv_sem):
        copy(like, like, pair_s, recv_sem, sibling).wait_recv()

    def left(like, send_sem):
        copy(like, like, send_sem, pair_r, sibling).wait_send()

    barrier = pltpu.get_barrier_semaphore()
    friends = [sibling, x_dev(1), x_dev(-1)]
    friends += [y_dev(by) for by in range(1, RING)] + [z_dev(by) for by in range(1, RING)]
    for friend in friends:
        pl.semaphore_signal(barrier, inc=1, device_id=friend, device_id_type=MESH)

    def rows_of(xx, cc):
        return pl.ds(pl.multiple_of((2 * xx + cc) * OWN, OWN), OWN)

    here = x_buf.at[rows_of(x, core)]
    local = [
        pltpu.make_async_copy(src, dst, in_sem.at[i])
        for i, (src, dst) in enumerate(
            [(w_query_hbm, w_query), (w_key_hbm, w_key), (w_value_hbm, w_value), (normed, here), (seg_hbm, seg), (grad_hbm, grad)]
        )
    ]
    for one in local:
        one.start()

    for one in local[:3]:
        one.wait()
    q_first, q_second = w_query[:, :HD].astype(F32), w_query[:, HD:].astype(F32)
    k_own, v_own = w_key[...].astype(F32), w_value[...].astype(F32)
    even = par == 0
    keep_q, give_q = jnp.where(even, q_first, q_second), jnp.where(even, q_second, q_first)
    keep_kv, give_kv = jnp.where(even, k_own, v_own), jnp.where(even, v_own, k_own)
    pair_out[...] = jnp.concatenate([give_q, give_kv], axis=0).astype(BF16)

    pl.semaphore_wait(barrier, len(friends))
    send(pair_out, pair_in, pair_s, pair_r, partner)
    for one in local[3:]:
        one.wait()
    send(here, here, x_s, x_r.at[0], x_dev(1))
    send(here, here, x_s, x_r.at[1], x_dev(-1))
    send(here, here, x_s, x_r.at[4], sibling)

    seg_f = seg[...].astype(F32)
    seg_col = jnp.transpose(jnp.broadcast_to(seg_f, (HD, TOK)))
    seg_col = jnp.concatenate([seg_col, seg_col], axis=1)
    key_at = lax.broadcasted_iota(jnp.int32, (TOK, TOK), 0)
    query_at = lax.broadcasted_iota(jnp.int32, (TOK, TOK), 1)
    mask[...] = jnp.where((key_at <= query_at) & (seg_col == seg_f), 1.0, 0.0).astype(F32)

    def pair_rows(pair):
        return pl.ds(pl.multiple_of(pair * PAIR, 16), PAIR)

    def unit_a(yy, zz):
        return w_buf.at[zz % 2, yy, pair_rows(zz // 2)]

    def unit_b(yy, zz):
        return w_buf.at[2 + zz % 2, yy, pair_rows(zz // 2)]

    arrived(pair_in, pair_r)
    got = pair_in[...].astype(F32)
    got_q, got_kv = got[:ROWS], got[ROWS:]
    w_buf[par, y, pair_rows(m), :] = jnp.where(
        even, jnp.concatenate([keep_q, got_q], axis=0), jnp.concatenate([got_q, keep_q], axis=0)
    ).astype(BF16)
    w_buf[2 + par, y, pair_rows(m), :] = jnp.where(
        even, jnp.concatenate([keep_kv, got_kv], axis=0), jnp.concatenate([got_kv, keep_kv], axis=0)
    ).astype(BF16)

    def first_hop(way, hop):
        by = SIGN[way]
        zz, yy = shift(z, -by * (hop - 1)), shift(y, -by * (hop - 1))
        slot = (way, hop - 1)
        send(unit_a(y, zz), unit_a(y, zz), turn_s, turn_r.at[(0,) + slot], z_dev(by))
        send(unit_b(yy, z), unit_b(yy, z), turn_s, turn_r.at[(1,) + slot], y_dev(by))

    def turn(entry):
        zz, yy = shift(z, ENTRIES[entry]), shift(y, ENTRIES[entry])
        for way in (RIGHT, LEFT):
            by, slot = SIGN[way], (way, 0, entry // GROUP)
            send(unit_a(y, zz), unit_a(y, zz), pass_s, a_r.at[slot], y_dev(by))
            send(unit_b(yy, z), unit_b(yy, z), pass_s, b_r.at[slot], z_dev(by))

    def first_arrived(hop):
        ways = (RIGHT, LEFT) if hop < 4 else (RIGHT,)
        for way in ways:
            for kind in range(2):
                arrived(pair_in, turn_r.at[kind, way, hop - 1])
            if hop + 1 <= (4 if way == RIGHT else 3):
                first_hop(way, hop + 1)
        for way in ways:
            turn(2 * hop - 1 + way)

    group_bytes = w_buf.at[0, 0]

    def pass_on(hop, group):
        for way in (RIGHT, LEFT):
            by = SIGN[way]
            yy, zz = shift(y, -by * hop), shift(z, -by * hop)
            entries = [GROUP * group + i for i in range(GROUP) if hop < 3 or i % 2 == way]
            slot = (way, hop, group) if hop < 3 else (RIGHT, 3, group)
            arrived(group_bytes, a_r.at[way, hop - 1, group])
            for entry in entries:
                unit = unit_a(yy, shift(z, ENTRIES[entry]))
                send(unit, unit, pass_s, a_r.at[slot], y_dev(by))
            arrived(group_bytes, b_r.at[way, hop - 1, group])
            for entry in entries:
                unit = unit_b(shift(y, ENTRIES[entry]), zz)
                send(unit, unit, pass_s, b_r.at[slot], z_dev(by))

    def pass_end(group):
        arrived(group_bytes, a_r.at[RIGHT, 3, group])
        arrived(group_bytes, b_r.at[RIGHT, 3, group])

    left_half, right_half = pl.ds(0, HALF), pl.ds(HALF, HALF)
    x_right, x_left, x_far = shift(x, 1, XS), shift(x, -1, XS), shift(x, 2, XS)

    def x_block(xx, columns=None):
        rows = rows_of(xx, core)
        return x_buf.at[rows] if columns is None else x_buf.at[rows, columns]

    def x_forward():
        arrived(here, x_r.at[0])
        send(x_block(x_left, left_half), x_block(x_left, left_half), x_s, x_r.at[2], x_dev(1))
        arrived(here, x_r.at[1])
        send(x_block(x_right, right_half), x_block(x_right, right_half), x_s, x_r.at[3], x_dev(-1))
        send(x_block(x_left), x_block(x_left), x_s, x_r.at[4], sibling)
        send(x_block(x_right), x_block(x_right), x_s, x_r.at[4], sibling)

    def x_finish():
        for way, columns in ((2, left_half), (3, right_half)):
            arrived(x_block(x_far, columns), x_r.at[way])
            send(x_block(x_far, columns), x_block(x_far, columns), x_s, x_r.at[4], sibling)
        arrived(x_buf.at[pl.ds(0, XS * OWN)], x_r.at[4])

    def flip(i, carry):
        columns = pl.ds(pl.multiple_of(i * CHUNK, HD), CHUNK)
        x_t[pl.ds(2 * i, 2)] = jnp.transpose(x_buf[:, columns]).reshape(2, 4, PAIR, TOK)
        return carry

    def flip_back(i, carry):
        x_p[i] = jnp.transpose(x_t[:, i].reshape(CHUNK, TOK))
        return carry

    def weights(kinds, p):
        return jnp.concatenate([w_buf[kind, pl.ds(2 * p, 2)].reshape(CHUNK, HD) for kind in kinds], axis=1)

    def q_product(p):
        return dot(x_buf[:, pl.ds(pl.multiple_of(p * CHUNK, HD), CHUNK)], weights((0, 1), p))

    def kv_product(p):
        both = [w_buf[kind, :, pair_rows(p), :].reshape(CHUNK, HD) for kind in (2, 3)]
        return dot(x_p[p], jnp.concatenate(both, axis=1))

    def order(position):
        near = 1 - 2 * ((position + 1) % 2)
        pair = position // 2
        return [pair, shift(pair, near, CHUNKS), shift(pair, -near, CHUNKS), shift(pair, 2, CHUNKS)]

    y_pairs, z_pairs = order(y), order(z)

    first_hop(RIGHT, 1)
    first_hop(LEFT, 1)
    turn(0)
    first_arrived(1)
    first_arrived(2)
    first_arrived(3)
    x_forward()
    pass_on(1, 0)
    first_arrived(4)
    pass_on(1, 1)
    pass_on(2, 0)
    x_finish()
    q_acc[...] = q_product(y_pairs[0])
    lax.fori_loop(0, CHUNKS, flip, 0)
    pass_on(2, 1)
    lax.fori_loop(0, CHUNKS, flip_back, 0)
    kv_acc[...] = kv_product(z_pairs[0])
    q_acc[...] += q_product(y_pairs[1])
    kv_acc[...] += kv_product(z_pairs[1])
    left(pair_out, pair_s)
    left(x_buf.at[pl.ds(0, 7 * OWN)], x_s)
    left(w_buf.at[0, pl.ds(0, 7), pl.ds(0, 2 * PAIR)], turn_s)
    pass_on(3, 0)
    pass_on(3, 1)
    q_acc[...] += q_product(y_pairs[2])
    kv_acc[...] += kv_product(z_pairs[2])
    pass_end(0)
    pass_end(1)
    kv = kv_acc[...] + kv_product(z_pairs[3])
    key, value = kv[:, :HD].astype(BF16), kv[:, HD:].astype(BF16)
    query = (q_acc[...] + q_product(y_pairs[3])).astype(BF16)

    allowed = mask[...] > 0.5
    probs, dprobs = [], []
    for h in range(2):
        scores = jnp.where(allowed, dot_nt(key, query[:, h * HD : (h + 1) * HD]) * QUERY_SCALE, MASKED)
        expo = jnp.exp(scores - jnp.max(scores, axis=0, keepdims=True))
        probs.append(expo * (1.0 / jnp.sum(expo, axis=0, keepdims=True)))
        dprobs.append(dot_nt(value, grad[:, h * HD : (h + 1) * HD]))
    rounded = [one.astype(BF16) for one in probs]
    grad_v = (dot(rounded[0], grad[:, :HD]) + dot(rounded[1], grad[:, HD:])).astype(BF16)

    for yy in range(RING):
        vw[yy // 2, yy % 2] = dot(x_t[yy].reshape(UNIT, TOK), grad_v).reshape(RING, ROWS, HD)

    def vw_y(yy, k):
        return vw[yy // 2, yy % 2, pl.ds(4 * (yy % 2) + 2 * k, 2)].reshape(PAIR, HD)

    def vw_z(zz, k):
        return vw[2 * k : 2 * k + 2, 1 - zz // 4, zz].reshape(PAIR, HD)

    def vw_step(step, long):
        for way in (RIGHT, LEFT):
            by, k = SIGN[way], way if long else 1 - way
            for own, position, sends, recvs, sems, device in (
                (vw_y, y, a_send, a_recv, va_r, y_dev(by)),
                (vw_z, z, b_send, b_recv, vb_r, z_dev(by)),
            ):
                total = own(shift(position, by * (5 - step)), k)
                if step > 2 or (step == 2 and long):
                    arrived(pair_in, sems.at[step - 2, k, way])
                    total = total + recvs[step - 2, k, way].astype(F32)
                slot = (step - 1, k, way)
                sends[slot] = total.astype(BF16)
                send(sends.at[slot], recvs.at[slot], v_s, sems.at[slot], device)

    y_first = z // 4 == y % 2

    def vw_turn():
        for base, own, position, recvs, sems in ((0, vw_y, y, a_recv, va_r), (4, vw_z, z, b_recv, vb_r)):
            for k in range(2):
                total = own(position, k)
                for way in (RIGHT, LEFT):
                    arrived(pair_in, sems.at[3, k, way])
                    total = total + recvs[3, k, way].astype(F32)
                total = total.reshape(2, ROWS, HD)
                line_sum[base + 2 * k : base + 2 * k + 2] = total
                padded = jnp.concatenate([total, jnp.zeros((2, PADDED - ROWS, HD), F32)], axis=1)
                line_send[base + 2 * k : base + 2 * k + 2] = padded.astype(BF16)
        for_line(True)

    def for_line(start):
        for i in range(4):
            zz, yy = 4 * (y % 2) + i, 2 * i + 1 - z // 4
            one = copy(line_send.at[i], line_recv.at[z], line_s.at[i], line_r, at(x, y, zz, core))
            two = copy(line_send.at[4 + i], line_recv.at[y], line_s.at[4 + i], line_r, at(x, yy, z, core))
            pl.when(zz != z)(one.start if start else one.wait_send)
            pl.when(yy != y)(two.start if start else two.wait_send)

    def vw_finish():
        arrived(line_recv.at[pl.ds(0, RING - 1)], line_r)
        position = jnp.where(y_first, z, y)
        total = line_sum[jnp.where(y_first, z % 4, 4 + y // 2)]
        for by in range(1, RING):
            total = total + line_recv[shift(position, by)].astype(F32)[:ROWS]
        value_grad[...] = total * float(TOK * RING * RING) ** (-0.5)

    vw_step(1, True)
    vw_step(2, False)

    dscores = []
    for h in range(2):
        delta = jnp.sum(rounded[h].astype(F32) * dprobs[h], axis=0, keepdims=True)
        dscores.append((probs[h] * (dprobs[h] - delta) * QUERY_SCALE).astype(BF16))
    key_t = jnp.transpose(key)
    for h in range(2):
        g_cat[:, h * HD : (h + 1) * HD] = jnp.transpose(dot(key_t, dscores[h])).astype(BF16)
    g_cat[:, 2 * HD : 3 * HD] = (dot(dscores[0], query[:, :HD]) + dot(dscores[1], query[:, HD:])).astype(BF16)
    g_cat[:, 3 * HD :] = grad_v

    def ig_part(q):
        both = dot_nt(g_cat[...], weights((0, 1, 2, 3), q)).astype(BF16)
        part[q] = both.reshape(XS, 2, OWN, CHUNK)
        send(part.at[q, :, other], sib.at[q], sib_s, sib_r.at[q], sibling)

    def chip_sum(q, xx):
        return part[q, xx, core].astype(F32) + sib[q, xx].astype(F32)

    def near(q, way):
        send(near_send.at[q, way], near_recv.at[q, way], near_s, near_r.at[q], x_dev(SIGN[way]))

    def ig_first(q):
        way = q % 2
        by = SIGN[way]
        arrived(sib.at[q], sib_r.at[q])
        far_send[q] = chip_sum(q, x_far).astype(BF16)
        send(far_send.at[q], far_recv.at[q], far_s, far_r.at[q], x_dev(by))
        near_send[q, 1 - way] = chip_sum(q, shift(x, -by, XS)).astype(BF16)
        near(q, 1 - way)

    def ig_second(q):
        way = q % 2
        arrived(far_recv.at[q], far_r.at[q])
        near_send[q, way] = (chip_sum(q, shift(x, SIGN[way], XS)) + far_recv[q].astype(F32)).astype(BF16)
        near(q, way)

    def ig_finish(q):
        total = chip_sum(q, x)
        arrived(near_recv.at[q], near_r.at[q])
        for way in (RIGHT, LEFT):
            total = total + near_recv[q, way].astype(F32)
        input_grad[:, q * CHUNK : (q + 1) * CHUNK] = total.astype(BF16)

    ig_part(0)
    ig_part(1)
    vw_step(2, True)
    ig_first(0)
    vw_step(3, False)
    ig_part(2)
    ig_first(1)
    ig_part(3)
    ig_first(2)
    vw_step(3, True)
    ig_first(3)
    vw_step(4, False)
    ig_second(0)
    ig_second(1)
    vw_step(4, True)
    ig_second(2)
    ig_second(3)
    vw_turn()
    left(w_buf.at[:, pl.ds(0, 7)], pass_s)
    left(w_buf.at[0, pl.ds(0, 7)], v_s)
    left(sib, sib_s)
    left(far_send, far_s)
    ig_finish(0)
    ig_finish(1)
    ig_finish(2)
    ig_finish(3)
    vw_finish()
    left(near_send, near_s)
    for_line(False)


def shards(*args):
    vmem = pl.BlockSpec(memory_space=pltpu.VMEM)
    dma = pltpu.SemaphoreType.DMA
    scratch = [
        pltpu.VMEM((1, TOK), jnp.int32),
        pltpu.VMEM((ROWS, 2 * HD), BF16),
        pltpu.VMEM((ROWS, HD), BF16),
        pltpu.VMEM((ROWS, HD), BF16),
        pltpu.VMEM((TOK, 2 * HD), BF16),
        pltpu.VMEM((TOK, D), BF16),
        pltpu.VMEM((RING, 4, PAIR, TOK), BF16),
        pltpu.VMEM((CHUNKS, TOK, CHUNK), BF16),
        pltpu.VMEM((4, RING, UNIT, HD), BF16),
        pltpu.VMEM((PAIR, HD), BF16),
        pltpu.VMEM((PAIR, HD), BF16),
        pltpu.VMEM((TOK, TOK), F32),
        pltpu.VMEM((TOK, 2 * HD), F32),
        pltpu.VMEM((TOK, 2 * HD), F32),
        pltpu.VMEM((TOK, 4 * HD), BF16),
        pltpu.VMEM((RING // 2, 2, RING, ROWS, HD), F32),
        pltpu.VMEM((4, 2, 2, PAIR, HD), BF16),
        pltpu.VMEM((4, 2, 2, PAIR, HD), BF16),
        pltpu.VMEM((4, 2, 2, PAIR, HD), BF16),
        pltpu.VMEM((4, 2, 2, PAIR, HD), BF16),
        pltpu.VMEM((RING, ROWS, HD), F32),
        pltpu.VMEM((RING, PADDED, HD), BF16),
        pltpu.VMEM((RING, PADDED, HD), BF16),
        pltpu.VMEM((CHUNKS, XS, 2, OWN, CHUNK), BF16),
        pltpu.VMEM((CHUNKS, XS, OWN, CHUNK), BF16),
        pltpu.VMEM((CHUNKS, OWN, CHUNK), BF16),
        pltpu.VMEM((CHUNKS, OWN, CHUNK), BF16),
        pltpu.VMEM((CHUNKS, 2, OWN, CHUNK), BF16),
        pltpu.VMEM((CHUNKS, 2, OWN, CHUNK), BF16),
        dma((6,)),
        dma(()), dma(()),
        dma(()), dma((5,)),
        dma(()), dma((2, 2, 4)),
        dma(()), dma((2, 4, 2)), dma((2, 4, 2)),
        dma(()), dma((4, 2, 2)), dma((4, 2, 2)),
        dma((RING,)), dma(()),
        dma(()), dma((CHUNKS,)),
        dma(()), dma((CHUNKS,)),
        dma(()), dma((CHUNKS,)),
    ]
    hbm = pl.BlockSpec(memory_space=pltpu.HBM)
    return pl.pallas_call(
        kernel,
        out_shape=(jax.ShapeDtypeStruct((OWN, D), BF16), jax.ShapeDtypeStruct((ROWS, HD), F32)),
        in_specs=[hbm] * 6,
        out_specs=(vmem, vmem),
        scratch_shapes=scratch,
        compiler_params=pltpu.CompilerParams(
            collective_id=0, has_side_effects=True, vmem_limit_bytes=50 * 1024 * 1024
        ),
        name="attention_backward",
    )(*[pltpu.with_memory_space_constraint(one, pltpu.HBM) for one in args])


def solution(mesh):
    return jax.shard_map(
        shards,
        mesh=mesh,
        in_specs=(
            P(("dp", "tensor"), None),
            P("dp", None),
            P("dp", "tensor"),
            P("dp", "tensor"),
            P("dp", "tensor"),
            P("dp", "tensor"),
        ),
        out_specs=(P(("dp", "tensor"), None), P("dp", "tensor")),
        check_vma=False,
    )
```

```python
import jax
import jax.numpy as jnp
from jax import lax
from jax.experimental import pallas as pl
from jax.experimental.pallas import tpu as pltpu
from jax.sharding import PartitionSpec as P

MESH = pl.DeviceIdType.MESH
F32 = jnp.float32
BF16 = jnp.bfloat16

D = 4608
HD = 128
TOK = 256
RING = 8
XS = 4
ROWS = 72
PAIR = 2 * ROWS
UNIT = RING * ROWS
HALF = D // 2
CHUNK = 2 * UNIT
CHUNKS = D // CHUNK
OWN = 32
PADDED = 80
ENTRIES = (0, -1, 1, -2, 2, -3, 3, -4)
GROUP = 2
QUERY_SCALE = 1.0 / 12.0
MASKED = -1e30
RIGHT, LEFT = 0, 1
SIGN = (1, -1)

NT = (((1,), (1,)), ((), ()))


def dot(a, b):
    return jnp.dot(a, b, preferred_element_type=F32)


def dot_nt(a, b):
    return lax.dot_general(a, b, NT, preferred_element_type=F32)


def kernel(
    normed, seg_hbm, w_query, w_key, w_value, grad_hbm,
    input_grad, value_grad,
    seg, grad, x_buf, x_t, x_p, w_raw, w_buf, mask, q_acc, kv_acc, g_cat,
    vw, v_send, v_recv, line_sum, line_send, line_recv,
    part, sib, far_send, far_recv, near_send, near_recv,
    in_sem, x_s, x_r, first_s, first_r, pass_s, a_r, b_r, a_end, b_end,
    v_s, v_r, line_s, line_r, sib_s, sib_r, far_s, far_r, near_s, near_r,
):
    dp, tensor = lax.axis_index("dp"), lax.axis_index("tensor")
    y, z, x, core = dp // RING, dp % RING, tensor // 2, tensor % 2
    other = 1 - core

    def at(xx, yy, zz, cc):
        return (yy * RING + zz, xx * 2 + cc)

    def shift(position, by, size=RING):
        return (position + by + size) % size

    def y_dev(by):
        return at(x, shift(y, by), z, core)

    def z_dev(by):
        return at(x, y, shift(z, by), core)

    def x_dev(by):
        return at(shift(x, by, XS), y, z, core)

    sibling = at(x, y, z, other)

    def copy(src, dst, send_sem, recv_sem, device):
        return pltpu.make_async_remote_copy(
            src_ref=src, dst_ref=dst, send_sem=send_sem, recv_sem=recv_sem, device_id=device, device_id_type=MESH
        )

    def send(src, dst, send_sem, recv_sem, device):
        copy(src, dst, send_sem, recv_sem, device).start()

    def arrived(like, recv_sem):
        copy(like, like, first_s, recv_sem, sibling).wait_recv()

    def left(like, send_sem):
        copy(like, like, send_sem, line_r, sibling).wait_send()

    barrier = pltpu.get_barrier_semaphore()
    friends = [sibling, x_dev(1), x_dev(-1)]
    friends += [y_dev(by) for by in range(1, RING)] + [z_dev(by) for by in range(1, RING)]
    for friend in friends:
        pl.semaphore_signal(barrier, inc=1, device_id=friend, device_id_type=MESH)

    def rows_of(xx, cc):
        return pl.ds(pl.multiple_of((2 * xx + cc) * OWN, OWN), OWN)

    here = x_buf.at[rows_of(x, core)]
    own = [w_query.at[:, :HD], w_query.at[:, HD:], w_key, w_value]
    own_a, own_b = w_raw.at[0, y, z], w_raw.at[1, y, z]
    local = [
        pltpu.make_async_copy(src, dst, in_sem.at[i])
        for src, dst, i in (
            (own[0], own_a.at[0], 0), (own[1], own_a.at[1], 0), (own[2], own_b.at[0], 1), (own[3], own_b.at[1], 1),
            (normed, here, 2), (seg_hbm, seg, 3), (grad_hbm, grad, 4),
        )
    ]
    for one in local:
        one.start()

    pl.semaphore_wait(barrier, len(friends))

    def send_own(route, entry, device):
        for i in range(2):
            send(own[2 * route + i], w_raw.at[route, y, z, i], first_s, first_r.at[route, entry], device)

    def turn_own():
        for i in range(2):
            for way in (RIGHT, LEFT):
                by = SIGN[way]
                send(own[i], own_a.at[i], pass_s, a_r.at[way, 0, 0], y_dev(by))
                send(own[2 + i], own_b.at[i], pass_s, b_r.at[way, 0, 0], z_dev(by))

    for entry in (1, 2):
        send_own(0, entry, z_dev(-ENTRIES[entry]))
        send_own(1, entry, y_dev(-ENTRIES[entry]))
    turn_own()
    for entry in range(3, 7):
        send_own(0, entry, z_dev(-ENTRIES[entry]))
        send_own(1, entry, y_dev(-ENTRIES[entry]))

    send(normed, here, x_s, x_r.at[0], x_dev(1))
    send(normed, here, x_s, x_r.at[1], x_dev(-1))
    send(normed, here, x_s, x_r.at[4], sibling)
    pltpu.make_async_copy(own_a, own_a, in_sem.at[0]).wait()
    pltpu.make_async_copy(own_b, own_b, in_sem.at[1]).wait()
    for one in local[4:]:
        one.wait()

    seg_f = seg[...].astype(F32)
    seg_col = jnp.transpose(jnp.broadcast_to(seg_f, (HD, TOK)))
    seg_col = jnp.concatenate([seg_col, seg_col], axis=1)
    key_at = lax.broadcasted_iota(jnp.int32, (TOK, TOK), 0)
    query_at = lax.broadcasted_iota(jnp.int32, (TOK, TOK), 1)
    mask[...] = jnp.where((key_at <= query_at) & (seg_col == seg_f), 1.0, 0.0).astype(F32)

    def unit_a(yy, zz):
        return w_raw.at[0, yy, zz]

    def unit_b(yy, zz):
        return w_raw.at[1, yy, zz]

    def turn(entry):
        zz, yy = shift(z, ENTRIES[entry]), shift(y, ENTRIES[entry])
        for way in (RIGHT, LEFT):
            by, slot = SIGN[way], (way, 0, entry // GROUP)
            send(unit_a(y, zz), unit_a(y, zz), pass_s, a_r.at[slot], y_dev(by))
            send(unit_b(yy, z), unit_b(yy, z), pass_s, b_r.at[slot], z_dev(by))

    def relay(way):
        by = SIGN[way]
        zz, yy = shift(z, -2 * by), shift(y, -2 * by)
        one, two = unit_a(y, zz).at[way], unit_b(yy, z).at[way]
        send(one, one, first_s, first_r.at[0, 7], z_dev(2 * by))
        send(two, two, first_s, first_r.at[1, 7], y_dev(2 * by))

    def first_arrived(entry):
        for route in range(2):
            arrived(own_a, first_r.at[route, entry])
        if entry in (3, 4):
            relay(entry - 3)
        turn(entry)

    group_bytes = w_raw.at[0, 0, pl.ds(0, GROUP)]

    def pass_on(hop, group):
        for way in (RIGHT, LEFT):
            by = SIGN[way]
            yy, zz = shift(y, -by * hop), shift(z, -by * hop)
            entries = [GROUP * group + i for i in range(GROUP) if hop < 3 or i % 2 == way]
            arrived(group_bytes, a_r.at[way, hop - 1, group])
            for entry in entries:
                unit = unit_a(yy, shift(z, ENTRIES[entry]))
                send(unit, unit, pass_s, a_r.at[way, hop, group] if hop < 3 else a_end.at[group], y_dev(by))
            arrived(group_bytes, b_r.at[way, hop - 1, group])
            for entry in entries:
                unit = unit_b(shift(y, ENTRIES[entry]), zz)
                send(unit, unit, pass_s, b_r.at[way, hop, group] if hop < 3 else b_end.at[group], z_dev(by))

    def pass_end(group):
        arrived(group_bytes, a_end.at[group])
        arrived(group_bytes, b_end.at[group])

    left_half, right_half = pl.ds(0, HALF), pl.ds(HALF, HALF)
    x_right, x_left, x_far = shift(x, 1, XS), shift(x, -1, XS), shift(x, 2, XS)

    def x_block(xx, columns=None):
        rows = rows_of(xx, core)
        return x_buf.at[rows] if columns is None else x_buf.at[rows, columns]

    def x_forward():
        arrived(here, x_r.at[0])
        send(x_block(x_left, left_half), x_block(x_left, left_half), x_s, x_r.at[2], x_dev(1))
        arrived(here, x_r.at[1])
        send(x_block(x_right, right_half), x_block(x_right, right_half), x_s, x_r.at[3], x_dev(-1))
        send(x_block(x_left), x_block(x_left), x_s, x_r.at[4], sibling)
        send(x_block(x_right), x_block(x_right), x_s, x_r.at[4], sibling)

    def x_finish():
        for way, columns in ((2, left_half), (3, right_half)):
            arrived(x_block(x_far, columns), x_r.at[way])
            send(x_block(x_far, columns), x_block(x_far, columns), x_s, x_r.at[4], sibling)
        arrived(x_buf.at[pl.ds(0, XS * OWN)], x_r.at[4])

    def flip(i, carry):
        columns = pl.ds(pl.multiple_of(i * CHUNK, HD), CHUNK)
        x_t[pl.ds(2 * i, 2)] = jnp.transpose(x_buf[:, columns]).reshape(2, 4, PAIR, TOK)
        return carry

    def flip_back(i, carry):
        x_p[i] = jnp.transpose(x_t[:, i].reshape(CHUNK, TOK))
        return carry

    def weights(kinds, p):
        return jnp.concatenate([w_buf[kind, pl.ds(2 * p, 2)].reshape(CHUNK, HD) for kind in kinds], axis=1)

    def q_product(p):
        both = []
        for i in range(2):
            block = w_raw[0, pl.ds(2 * p, 2), :, i].astype(F32).reshape(CHUNK, HD).astype(BF16)
            w_buf[i, pl.ds(2 * p, 2)] = block.reshape(2, UNIT, HD)
            both.append(block)
        return dot(x_buf[:, pl.ds(pl.multiple_of(p * CHUNK, HD), CHUNK)], jnp.concatenate(both, axis=1))

    def kv_product(p):
        both = []
        for i in range(2):
            block = w_raw[1, :, pl.ds(2 * p, 2), i].astype(F32).reshape(CHUNK, HD).astype(BF16)
            w_buf[2 + i, :, pl.ds(pl.multiple_of(p * PAIR, 16), PAIR), :] = block.reshape(RING, PAIR, HD)
            both.append(block)
        return dot(x_p[p], jnp.concatenate(both, axis=1))

    def order(position):
        near = 1 - 2 * ((position + 1) % 2)
        pair = position // 2
        return [pair, shift(pair, near, CHUNKS), shift(pair, -near, CHUNKS), shift(pair, 2, CHUNKS)]

    y_pairs, z_pairs = order(y), order(z)

    for entry in range(1, 7):
        first_arrived(entry)
    pass_on(1, 0)
    first_arrived(7)
    pass_on(1, 1)
    x_forward()
    pass_on(1, 2)
    pass_on(2, 0)
    pass_on(1, 3)
    pass_on(2, 1)
    pass_on(2, 2)
    pass_on(3, 0)
    pass_on(2, 3)
    x_finish()
    q_acc[...] = q_product(y_pairs[0])
    pass_on(3, 1)
    lax.fori_loop(0, CHUNKS, flip, 0)
    pass_on(3, 2)
    lax.fori_loop(0, CHUNKS, flip_back, 0)
    pass_on(3, 3)
    left(w_raw.at[:, 0, pl.ds(0, 7)], first_s)
    left(x_buf.at[pl.ds(0, 7 * OWN)], x_s)
    kv_acc[...] = kv_product(z_pairs[0])
    q_acc[...] += q_product(y_pairs[1])
    kv_acc[...] += kv_product(z_pairs[1])
    q_acc[...] += q_product(y_pairs[2])
    kv_acc[...] += kv_product(z_pairs[2])
    for group in range(RING // GROUP):
        pass_end(group)
    kv = kv_acc[...] + kv_product(z_pairs[3])
    key, value = kv[:, :HD].astype(BF16), kv[:, HD:].astype(BF16)
    query = (q_acc[...] + q_product(y_pairs[3])).astype(BF16)

    allowed = mask[...] > 0.5
    probs, dprobs = [], []
    for h in range(2):
        scores = jnp.where(allowed, dot_nt(key, query[:, h * HD : (h + 1) * HD]) * QUERY_SCALE, MASKED)
        expo = jnp.exp(scores - jnp.max(scores, axis=0, keepdims=True))
        probs.append(expo * (1.0 / jnp.sum(expo, axis=0, keepdims=True)))
        dprobs.append(dot_nt(value, grad[:, h * HD : (h + 1) * HD]))
    rounded = [one.astype(BF16) for one in probs]
    grad_v = (dot(rounded[0], grad[:, :HD]) + dot(rounded[1], grad[:, HD:])).astype(BF16)

    for yy in range(RING):
        vw[yy // 2, yy % 2] = dot(x_t[yy].reshape(UNIT, TOK), grad_v).reshape(RING, ROWS, HD)

    def vw_y(yy, k):
        return vw[yy // 2, yy % 2, pl.ds(4 * (yy % 2) + 2 * k, 2)].reshape(PAIR, HD)

    def vw_z(zz, k):
        return vw[2 * k : 2 * k + 2, 1 - zz // 4, zz].reshape(PAIR, HD)

    routes = ((vw_y, y, y_dev), (vw_z, z, z_dev))

    def vw_send(route, way, slot, device):
        v_s_r = v_r.at[route, way, slot]
        send(v_send.at[route, way, slot], v_recv.at[route, way, slot], v_s, v_s_r, device)

    def vw_first():
        for way in (RIGHT, LEFT):
            by = SIGN[way]
            for route, (own_part, position, device) in enumerate(routes):
                v_send[route, way, 0] = own_part(shift(position, 4 * by), way).astype(BF16)
                vw_send(route, way, 0, device(2 * by))
                for slot, k in ((1, 1 - way), (2, way)):
                    v_send[route, way, slot] = own_part(shift(position, 3 * by), k).astype(BF16)
                    vw_send(route, way, slot, device(by))

    def vw_near():
        for way in (RIGHT, LEFT):
            by = SIGN[way]
            for route, (own_part, position, device) in enumerate(routes):
                for k in range(2):
                    v_send[route, way, 5 + k] = own_part(shift(position, by), k).astype(BF16)
                    vw_send(route, way, 5 + k, device(by))

    def vw_second():
        for way in (RIGHT, LEFT):
            by = SIGN[way]
            for route, (own_part, position, device) in enumerate(routes):
                for slot, k, gets in ((3, 1 - way, (1,)), (4, way, (0, 2))):
                    total = own_part(shift(position, 2 * by), k)
                    for got in gets:
                        arrived(v_send.at[0, 0, 0], v_r.at[route, way, got])
                        total = total + v_recv[route, way, got].astype(F32)
                    v_send[route, way, slot] = total.astype(BF16)
                    vw_send(route, way, slot, device(2 * by))

    y_first = z // 4 == y % 2

    def vw_turn():
        for route, (own_part, position, _) in enumerate(routes):
            for k in range(2):
                total = own_part(position, k)
                for way in (RIGHT, LEFT):
                    for slot in (5 + k, 4 if k == way else 3):
                        arrived(v_send.at[0, 0, 0], v_r.at[route, way, slot])
                        total = total + v_recv[route, way, slot].astype(F32)
                total = total.reshape(2, ROWS, HD)
                at_rows = pl.ds(4 * route + 2 * k, 2)
                line_sum[at_rows] = total
                padded = jnp.concatenate([total, jnp.zeros((2, PADDED - ROWS, HD), F32)], axis=1)
                line_send[at_rows] = padded.astype(BF16)
        for i in range(4):
            zz, yy = 4 * (y % 2) + i, 2 * i + 1 - z // 4
            one = copy(line_send.at[i], line_recv.at[z], line_s, line_r, at(x, y, zz, core))
            two = copy(line_send.at[4 + i], line_recv.at[y], line_s, line_r, at(x, yy, z, core))
            pl.when(zz != z)(one.start)
            pl.when(yy != y)(two.start)

    def vw_finish():
        arrived(line_recv.at[pl.ds(0, RING - 1)], line_r)
        position = jnp.where(y_first, z, y)
        total = line_sum[jnp.where(y_first, z % 4, 4 + y // 2)]
        for by in range(1, RING):
            total = total + line_recv[shift(position, by)].astype(F32)[:ROWS]
        value_grad[...] = total * float(TOK * RING * RING) ** (-0.5)

    vw_first()
    vw_near()

    dscores = []
    for h in range(2):
        delta = jnp.sum(rounded[h].astype(F32) * dprobs[h], axis=0, keepdims=True)
        dscores.append((probs[h] * (dprobs[h] - delta) * QUERY_SCALE).astype(BF16))
    key_t = jnp.transpose(key)
    for h in range(2):
        g_cat[:, h * HD : (h + 1) * HD] = jnp.transpose(dot(key_t, dscores[h])).astype(BF16)
    g_cat[:, 2 * HD : 3 * HD] = (dot(dscores[0], query[:, :HD]) + dot(dscores[1], query[:, HD:])).astype(BF16)
    g_cat[:, 3 * HD :] = grad_v

    def ig_part(q):
        both = dot_nt(g_cat[...], weights((0, 1, 2, 3), q)).astype(BF16)
        part[q] = both.reshape(XS, 2, OWN, CHUNK)
        send(part.at[q, :, other], sib.at[q], sib_s, sib_r.at[q], sibling)

    def chip_sum(q, xx):
        return part[q, xx, core].astype(F32) + sib[q, xx].astype(F32)

    def near(q, way):
        send(near_send.at[q, way], near_recv.at[q, way], near_s, near_r.at[q], x_dev(SIGN[way]))

    def ig_far(q):
        arrived(sib.at[q], sib_r.at[q])
        far_send[q] = chip_sum(q, x_far).astype(BF16)
        send(far_send.at[q], far_recv.at[q], far_s, far_r.at[q], x_dev(SIGN[q % 2]))

    def ig_near(q):
        way = 1 - q % 2
        near_send[q, way] = chip_sum(q, shift(x, SIGN[way], XS)).astype(BF16)
        near(q, way)

    def ig_second(q):
        way = q % 2
        arrived(far_recv.at[q], far_r.at[q])
        near_send[q, way] = (chip_sum(q, shift(x, SIGN[way], XS)) + far_recv[q].astype(F32)).astype(BF16)
        near(q, way)

    def ig_finish(q):
        total = chip_sum(q, x)
        arrived(near_recv.at[q], near_r.at[q])
        for way in (RIGHT, LEFT):
            total = total + near_recv[q, way].astype(F32)
        input_grad[:, q * CHUNK : (q + 1) * CHUNK] = total.astype(BF16)

    ig_part(0)
    ig_part(1)
    ig_part(2)
    ig_far(0)
    ig_part(3)
    ig_far(1)
    ig_far(2)
    ig_near(0)
    ig_near(1)
    ig_far(3)
    ig_near(2)
    ig_near(3)
    vw_second()
    ig_second(0)
    ig_second(1)
    ig_second(2)
    ig_second(3)
    vw_turn()
    left(w_raw.at[:, :, pl.ds(0, 7)], pass_s)
    left(v_send, v_s)
    left(sib, sib_s)
    left(far_send, far_s)
    ig_finish(0)
    ig_finish(1)
    vw_finish()
    left(line_recv.at[pl.ds(0, RING - 1)], line_s)
    ig_finish(2)
    ig_finish(3)
    left(near_send, near_s)


def shards(*args):
    vmem = pl.BlockSpec(memory_space=pltpu.VMEM)
    dma = pltpu.SemaphoreType.DMA
    scratch = [
        pltpu.VMEM((1, TOK), jnp.int32),
        pltpu.VMEM((TOK, 2 * HD), BF16),
        pltpu.VMEM((TOK, D), BF16),
        pltpu.VMEM((RING, 4, PAIR, TOK), BF16),
        pltpu.VMEM((CHUNKS, TOK, CHUNK), BF16),
        pltpu.VMEM((2, RING, RING, 2, ROWS, HD), BF16),
        pltpu.VMEM((4, RING, UNIT, HD), BF16),
        pltpu.VMEM((TOK, TOK), F32),
        pltpu.VMEM((TOK, 2 * HD), F32),
        pltpu.VMEM((TOK, 2 * HD), F32),
        pltpu.VMEM((TOK, 4 * HD), BF16),
        pltpu.VMEM((RING // 2, 2, RING, ROWS, HD), F32),
        pltpu.VMEM((2, 2, 7, PAIR, HD), BF16),
        pltpu.VMEM((2, 2, 7, PAIR, HD), BF16),
        pltpu.VMEM((RING, ROWS, HD), F32),
        pltpu.VMEM((RING, PADDED, HD), BF16),
        pltpu.VMEM((RING, PADDED, HD), BF16),
        pltpu.VMEM((CHUNKS, XS, 2, OWN, CHUNK), BF16),
        pltpu.VMEM((CHUNKS, XS, OWN, CHUNK), BF16),
        pltpu.VMEM((CHUNKS, OWN, CHUNK), BF16),
        pltpu.VMEM((CHUNKS, OWN, CHUNK), BF16),
        pltpu.VMEM((CHUNKS, 2, OWN, CHUNK), BF16),
        pltpu.VMEM((CHUNKS, 2, OWN, CHUNK), BF16),
        dma((5,)),
        dma(()), dma((5,)),
        dma(()), dma((2, RING)),
        dma(()), dma((2, 3, 4)), dma((2, 3, 4)), dma((4,)), dma((4,)),
        dma(()), dma((2, 2, 7)),
        dma(()), dma(()),
        dma(()), dma((CHUNKS,)),
        dma(()), dma((CHUNKS,)),
        dma(()), dma((CHUNKS,)),
    ]
    hbm = pl.BlockSpec(memory_space=pltpu.HBM)
    return pl.pallas_call(
        kernel,
        out_shape=(jax.ShapeDtypeStruct((OWN, D), BF16), jax.ShapeDtypeStruct((ROWS, HD), F32)),
        in_specs=[hbm] * 6,
        out_specs=(vmem, vmem),
        scratch_shapes=scratch,
        compiler_params=pltpu.CompilerParams(
            collective_id=0, has_side_effects=True, vmem_limit_bytes=50 * 1024 * 1024
        ),
        name="attention_backward",
    )(*[pltpu.with_memory_space_constraint(one, pltpu.HBM) for one in args])


def solution(mesh):
    return jax.shard_map(
        shards,
        mesh=mesh,
        in_specs=(
            P(("dp", "tensor"), None),
            P("dp", None),
            P("dp", "tensor"),
            P("dp", "tensor"),
            P("dp", "tensor"),
            P("dp", "tensor"),
        ),
        out_specs=(P(("dp", "tensor"), None), P("dp", "tensor")),
        check_vma=False,
    )
```

```python
import jax
import jax.numpy as jnp
from jax import lax
from jax.experimental import pallas as pl
from jax.experimental.pallas import tpu as pltpu
from jax.sharding import PartitionSpec as P

MESH = pl.DeviceIdType.MESH
F32 = jnp.float32
BF16 = jnp.bfloat16

D = 4608
HD = 128
TOK = 256
RING = 8
XS = 4
ROWS = 72
PAIR = 2 * ROWS
UNIT = RING * ROWS
HALF = D // 2
CHUNK = 2 * UNIT
CHUNKS = D // CHUNK
OWN = 32
PADDED = 80
ENTRIES = (0, -1, 1, -2, 2, -3, 3, -4)
GROUP = 2
QUERY_SCALE = 1.0 / 12.0
MASKED = -1e30
RIGHT, LEFT = 0, 1
SIGN = (1, -1)

NT = (((1,), (1,)), ((), ()))


def dot(a, b):
    return jnp.dot(a, b, preferred_element_type=F32)


def dot_nt(a, b):
    return lax.dot_general(a, b, NT, preferred_element_type=F32)


def kernel(
    normed, seg_hbm, w_query, w_key, w_value, grad_hbm,
    input_grad, value_grad,
    seg, grad, x_buf, x_t, x_p, w_raw, w_buf, mask, q_acc, kv_acc, g_cat,
    vw, v_send, v_recv, line_sum, line_send, line_recv,
    part, sib, far_send, far_recv, near_send, near_recv,
    in_sem, x_s, x_r, first_s, first_r, pass_s, a_r, b_r, end_r,
    v_s, v_r, v_end, line_s, line_r, sib_s, sib_r, far_s, far_r, near_s, near_r,
):
    dp, tensor = lax.axis_index("dp"), lax.axis_index("tensor")
    y, z, x, core = dp // RING, dp % RING, tensor // 2, tensor % 2
    other = 1 - core

    def at(xx, yy, zz, cc):
        return (yy * RING + zz, xx * 2 + cc)

    def shift(position, by, size=RING):
        return (position + by + size) % size

    def y_dev(by):
        return at(x, shift(y, by), z, core)

    def z_dev(by):
        return at(x, y, shift(z, by), core)

    def x_dev(by):
        return at(shift(x, by, XS), y, z, core)

    sibling = at(x, y, z, other)

    def copy(src, dst, send_sem, recv_sem, device):
        return pltpu.make_async_remote_copy(
            src_ref=src, dst_ref=dst, send_sem=send_sem, recv_sem=recv_sem, device_id=device, device_id_type=MESH
        )

    def send(src, dst, send_sem, recv_sem, device):
        copy(src, dst, send_sem, recv_sem, device).start()

    def arrived(like, recv_sem):
        copy(like, like, first_s, recv_sem, sibling).wait_recv()

    def left(like, send_sem):
        copy(like, like, send_sem, line_r, sibling).wait_send()

    barrier = pltpu.get_barrier_semaphore()
    friends = [sibling, x_dev(1), x_dev(-1)]
    friends += [device(by) for device in (y_dev, z_dev) for by in (1, -1, 2, -2)]
    for friend in friends:
        pl.semaphore_signal(barrier, inc=1, device_id=friend, device_id_type=MESH)

    def rows_of(xx, cc):
        return pl.ds(pl.multiple_of((2 * xx + cc) * OWN, OWN), OWN)

    here = x_buf.at[rows_of(x, core)]
    own = [w_query.at[:, :HD], w_query.at[:, HD:], w_key, w_value]
    own_a, own_b = w_raw.at[0, y, z], w_raw.at[1, y, z]
    local = [
        pltpu.make_async_copy(src, dst, in_sem.at[i])
        for src, dst, i in (
            (own[0], own_a.at[0], 0), (own[1], own_a.at[1], 0), (own[2], own_b.at[0], 1), (own[3], own_b.at[1], 1),
            (normed, here, 2), (seg_hbm, seg, 3), (grad_hbm, grad, 4),
        )
    ]
    for one in local:
        one.start()

    pl.semaphore_wait(barrier, len(friends))

    def send_own(route, entry, device):
        for i in range(2):
            send(own[2 * route + i], w_raw.at[route, y, z, i], first_s, first_r.at[route, entry], device)

    def turn_own():
        for i in range(2):
            for way in (RIGHT, LEFT):
                by = SIGN[way]
                send(own[i], own_a.at[i], pass_s, a_r.at[way, 0, 0], y_dev(by))
                send(own[2 + i], own_b.at[i], pass_s, b_r.at[way, 0, 0], z_dev(by))

    for entry in (1, 2):
        send_own(0, entry, z_dev(-ENTRIES[entry]))
        send_own(1, entry, y_dev(-ENTRIES[entry]))
    turn_own()
    for entry in (3, 4):
        send_own(0, entry, z_dev(-ENTRIES[entry]))
        send_own(1, entry, y_dev(-ENTRIES[entry]))

    send(normed, here, x_s, x_r.at[0], x_dev(1))
    send(normed, here, x_s, x_r.at[1], x_dev(-1))
    send(normed, here, x_s, x_r.at[4], sibling)
    pltpu.make_async_copy(own_a, own_a, in_sem.at[0]).wait()
    pltpu.make_async_copy(own_b, own_b, in_sem.at[1]).wait()
    for one in local[4:]:
        one.wait()

    seg_f = seg[...].astype(F32)
    seg_col = jnp.transpose(jnp.broadcast_to(seg_f, (HD, TOK)))
    seg_col = jnp.concatenate([seg_col, seg_col], axis=1)
    key_at = lax.broadcasted_iota(jnp.int32, (TOK, TOK), 0)
    query_at = lax.broadcasted_iota(jnp.int32, (TOK, TOK), 1)
    mask[...] = jnp.where((key_at <= query_at) & (seg_col == seg_f), 1.0, 0.0).astype(F32)

    def unit_a(yy, zz):
        return w_raw.at[0, yy, zz]

    def unit_b(yy, zz):
        return w_raw.at[1, yy, zz]

    def turn(entry):
        zz, yy = shift(z, ENTRIES[entry]), shift(y, ENTRIES[entry])
        for way in (RIGHT, LEFT):
            by, slot = SIGN[way], (way, 0, entry // GROUP)
            send(unit_a(y, zz), unit_a(y, zz), pass_s, a_r.at[slot], y_dev(by))
            send(unit_b(yy, z), unit_b(yy, z), pass_s, b_r.at[slot], z_dev(by))

    def relay(way):
        by = SIGN[way]
        one, two = unit_a(y, shift(z, -2 * by)), unit_b(shift(y, -2 * by), z)
        for route, unit, device in ((0, one, z_dev), (1, two, y_dev)):
            send(unit, unit, first_s, first_r.at[route, 5 + way], device(by))
            send(unit.at[way], unit.at[way], first_s, first_r.at[route, 7], device(2 * by))

    def first_arrived(entry):
        for route in range(2):
            arrived(own_a, first_r.at[route, entry])
        if entry in (3, 4):
            relay(entry - 3)
        turn(entry)

    group_bytes = w_raw.at[0, 0, pl.ds(0, GROUP)]

    def pass_on(hop, group):
        for way in (RIGHT, LEFT):
            by = SIGN[way]
            yy, zz = shift(y, -by * hop), shift(z, -by * hop)
            entries = [GROUP * group + i for i in range(GROUP) if hop < 3 or i % 2 == way]
            arrived(group_bytes, a_r.at[way, hop - 1, group])
            for entry in entries:
                unit = unit_a(yy, shift(z, ENTRIES[entry]))
                send(unit, unit, pass_s, a_r.at[way, hop, group] if hop < 3 else end_r.at[0], y_dev(by))
            arrived(group_bytes, b_r.at[way, hop - 1, group])
            for entry in entries:
                unit = unit_b(shift(y, ENTRIES[entry]), zz)
                send(unit, unit, pass_s, b_r.at[way, hop, group] if hop < 3 else end_r.at[1], z_dev(by))

    def pass_end():
        arrived(w_raw.at[0, 0], end_r.at[0])
        arrived(w_raw.at[0, 0], end_r.at[1])

    left_half, right_half = pl.ds(0, HALF), pl.ds(HALF, HALF)
    x_right, x_left, x_far = shift(x, 1, XS), shift(x, -1, XS), shift(x, 2, XS)

    def x_block(xx, columns=None):
        rows = rows_of(xx, core)
        return x_buf.at[rows] if columns is None else x_buf.at[rows, columns]

    def x_forward():
        arrived(here, x_r.at[0])
        send(x_block(x_left, left_half), x_block(x_left, left_half), x_s, x_r.at[2], x_dev(1))
        arrived(here, x_r.at[1])
        send(x_block(x_right, right_half), x_block(x_right, right_half), x_s, x_r.at[3], x_dev(-1))
        send(x_block(x_left), x_block(x_left), x_s, x_r.at[4], sibling)
        send(x_block(x_right), x_block(x_right), x_s, x_r.at[4], sibling)

    def x_share():
        for way, columns in ((2, left_half), (3, right_half)):
            arrived(x_block(x_far, columns), x_r.at[way])
            send(x_block(x_far, columns), x_block(x_far, columns), x_s, x_r.at[4], sibling)

    def x_finish():
        arrived(x_buf.at[pl.ds(0, XS * OWN)], x_r.at[4])

    def flip(i, carry):
        columns = pl.ds(pl.multiple_of(i * CHUNK, HD), CHUNK)
        x_t[pl.ds(2 * i, 2)] = jnp.transpose(x_buf[:, columns]).reshape(2, 4, PAIR, TOK)
        return carry

    def flip_back(i, carry):
        x_p[i] = jnp.transpose(x_t[:, i].reshape(CHUNK, TOK))
        return carry

    def weights(kinds, p):
        return jnp.concatenate([w_buf[kind, pl.ds(2 * p, 2)].reshape(CHUNK, HD) for kind in kinds], axis=1)

    def q_product(p):
        both = []
        for i in range(2):
            block = w_raw[0, pl.ds(2 * p, 2), :, i].astype(F32).reshape(CHUNK, HD).astype(BF16)
            w_buf[i, pl.ds(2 * p, 2)] = block.reshape(2, UNIT, HD)
            both.append(block)
        return dot(x_buf[:, pl.ds(pl.multiple_of(p * CHUNK, HD), CHUNK)], jnp.concatenate(both, axis=1))

    def kv_product(p):
        both = []
        for i in range(2):
            block = w_raw[1, :, pl.ds(2 * p, 2), i].astype(F32).reshape(CHUNK, HD).astype(BF16)
            w_buf[2 + i, :, pl.ds(pl.multiple_of(p * PAIR, 16), PAIR), :] = block.reshape(RING, PAIR, HD)
            both.append(block)
        return dot(x_p[p], jnp.concatenate(both, axis=1))

    def order(position):
        near = 1 - 2 * ((position + 1) % 2)
        pair = position // 2
        return [pair, shift(pair, near, CHUNKS), shift(pair, -near, CHUNKS), shift(pair, 2, CHUNKS)]

    y_pairs, z_pairs = order(y), order(z)

    first_arrived(1)
    first_arrived(2)
    first_arrived(3)
    first_arrived(4)
    pass_on(1, 0)
    first_arrived(5)
    first_arrived(6)
    x_forward()
    first_arrived(7)
    pass_on(1, 1)
    pass_on(2, 0)
    pass_on(1, 2)
    pass_on(1, 3)
    pass_on(2, 1)
    pass_on(3, 0)
    x_share()
    pass_on(2, 2)
    pass_on(2, 3)
    x_finish()
    q_acc[...] = q_product(y_pairs[0])
    pass_on(3, 1)
    pass_on(3, 2)
    lax.fori_loop(0, CHUNKS, flip, 0)
    pass_on(3, 3)
    left(w_raw.at[:, 0, pl.ds(0, 7)], first_s)
    left(x_buf.at[pl.ds(0, 7 * OWN)], x_s)
    lax.fori_loop(0, CHUNKS, flip_back, 0)
    kv_acc[...] = kv_product(z_pairs[0])
    q_acc[...] += q_product(y_pairs[1])
    kv_acc[...] += kv_product(z_pairs[1])
    q_acc[...] += q_product(y_pairs[2])
    kv_acc[...] += kv_product(z_pairs[2])
    pass_end()
    kv = kv_acc[...] + kv_product(z_pairs[3])
    key, value = kv[:, :HD].astype(BF16), kv[:, HD:].astype(BF16)
    query = (q_acc[...] + q_product(y_pairs[3])).astype(BF16)

    allowed = mask[...] > 0.5
    probs, dprobs = [], []
    for h in range(2):
        scores = jnp.where(allowed, dot_nt(key, query[:, h * HD : (h + 1) * HD]) * QUERY_SCALE, MASKED)
        expo = jnp.exp(scores - jnp.max(scores, axis=0, keepdims=True))
        probs.append(expo * (1.0 / jnp.sum(expo, axis=0, keepdims=True)))
        dprobs.append(dot_nt(value, grad[:, h * HD : (h + 1) * HD]))
    rounded = [one.astype(BF16) for one in probs]
    grad_v = (dot(rounded[0], grad[:, :HD]) + dot(rounded[1], grad[:, HD:])).astype(BF16)

    for yy in range(RING):
        vw[yy // 2, yy % 2] = dot(x_t[yy].reshape(UNIT, TOK), grad_v).reshape(RING, ROWS, HD)

    def vw_y(yy, k):
        return vw[yy // 2, yy % 2, pl.ds(4 * (yy % 2) + 2 * k, 2)].reshape(PAIR, HD)

    def vw_z(zz, k):
        return vw[2 * k : 2 * k + 2, 1 - zz // 4, zz].reshape(PAIR, HD)

    routes = ((vw_y, y, y_dev), (vw_z, z, z_dev))

    def vw_send(route, way, slot, sem, device, count=1):
        one, two = [ref.at[route, way, pl.ds(slot, count)] for ref in (v_send, v_recv)]
        send(one, two, v_s, sem, device)

    def vw_first():
        for way in (RIGHT, LEFT):
            for route, (own_part, position, device) in enumerate(routes):
                by = SIGN[way]
                v_send[route, way, 2] = own_part(shift(position, 4 * by), way).astype(BF16)
                vw_send(route, way, 2, v_r.at[route, way, 1], device(2 * by))
        for way in (RIGHT, LEFT):
            for route, (own_part, position, device) in enumerate(routes):
                by = SIGN[way]
                for slot, k in ((0, 1 - way), (1, way)):
                    v_send[route, way, slot] = own_part(shift(position, 3 * by), k).astype(BF16)
                    vw_send(route, way, slot, v_r.at[route, way, slot], device(by))
        for way in (RIGHT, LEFT):
            for route, (own_part, position, device) in enumerate(routes):
                by = SIGN[way]
                for k in range(2):
                    v_send[route, way, 5 + k] = own_part(shift(position, by), k).astype(BF16)
                vw_send(route, way, 5, v_end.at[route], device(by), 2)

    def vw_second(long):
        for way in (RIGHT, LEFT):
            for route, (own_part, position, device) in enumerate(routes):
                by, k = SIGN[way], way if long else 1 - way
                total = own_part(shift(position, 2 * by), k)
                gets = (1, 2) if long else (0,)
                arrived(v_send.at[0, 0, pl.ds(0, len(gets))], v_r.at[route, way, int(long)])
                for got in gets:
                    total = total + v_recv[route, way, got].astype(F32)
                v_send[route, way, 3 + k] = total.astype(BF16)
                vw_send(route, way, 3 + k, v_end.at[route], device(2 * by))

    y_first = z // 4 == y % 2

    def vw_turn():
        for route, (own_part, position, _) in enumerate(routes):
            arrived(v_send.at[0, :, pl.ds(3, 4)], v_end.at[route])
            for k in range(2):
                total = own_part(position, k)
                for way in (RIGHT, LEFT):
                    for slot in (5 + k, 3 + k):
                        total = total + v_recv[route, way, slot].astype(F32)
                total = total.reshape(2, ROWS, HD)
                at_rows = pl.ds(4 * route + 2 * k, 2)
                line_sum[at_rows] = total
                padded = jnp.concatenate([total, jnp.zeros((2, PADDED - ROWS, HD), F32)], axis=1)
                line_send[at_rows] = padded.astype(BF16)
        for i in range(4):
            zz, yy = 4 * (y % 2) + i, 2 * i + 1 - z // 4
            one = copy(line_send.at[i], line_recv.at[z], line_s, line_r, at(x, y, zz, core))
            two = copy(line_send.at[4 + i], line_recv.at[y], line_s, line_r, at(x, yy, z, core))
            pl.when(zz != z)(one.start)
            pl.when(yy != y)(two.start)

    def vw_finish():
        arrived(line_recv.at[pl.ds(0, RING - 1)], line_r)
        position = jnp.where(y_first, z, y)
        total = line_sum[jnp.where(y_first, z % 4, 4 + y // 2)]
        for by in range(1, RING):
            total = total + line_recv[shift(position, by)].astype(F32)[:ROWS]
        value_grad[...] = total * float(TOK * RING * RING) ** (-0.5)

    vw_first()

    dscores = []
    for h in range(2):
        delta = jnp.sum(rounded[h].astype(F32) * dprobs[h], axis=0, keepdims=True)
        dscores.append((probs[h] * (dprobs[h] - delta) * QUERY_SCALE).astype(BF16))
    key_t = jnp.transpose(key)
    for h in range(2):
        g_cat[:, h * HD : (h + 1) * HD] = jnp.transpose(dot(key_t, dscores[h])).astype(BF16)
    g_cat[:, 2 * HD : 3 * HD] = (dot(dscores[0], query[:, :HD]) + dot(dscores[1], query[:, HD:])).astype(BF16)
    g_cat[:, 3 * HD :] = grad_v

    def ig_part(q):
        both = dot_nt(g_cat[...], weights((0, 1, 2, 3), q)).astype(BF16)
        part[q] = both.reshape(XS, 2, OWN, CHUNK)
        for xx, sem in ((x_far, 0), (x_right, 1), (x_left, 1), (x, 1)):
            send(part.at[q, xx, other], sib.at[q, xx], sib_s, sib_r.at[sem, q], sibling)

    def chip_sum(q, xx):
        return part[q, xx, core].astype(F32) + sib[q, xx].astype(F32)

    def near(q, way):
        send(near_send.at[q, way], near_recv.at[q, way], near_s, near_r.at[q], x_dev(SIGN[way]))

    def ig_far(q):
        arrived(sib.at[q, 0], sib_r.at[0, q])
        far_send[q] = chip_sum(q, x_far).astype(BF16)
        send(far_send.at[q], far_recv.at[q], far_s, far_r.at[q], x_dev(SIGN[q % 2]))

    def ig_near(q):
        way = 1 - q % 2
        arrived(sib.at[q, pl.ds(0, 3)], sib_r.at[1, q])
        near_send[q, way] = chip_sum(q, shift(x, SIGN[way], XS)).astype(BF16)
        near(q, way)

    def ig_second(q):
        way = q % 2
        arrived(far_recv.at[q], far_r.at[q])
        near_send[q, way] = (chip_sum(q, shift(x, SIGN[way], XS)) + far_recv[q].astype(F32)).astype(BF16)
        near(q, way)

    def ig_finish(q):
        total = chip_sum(q, x)
        arrived(near_recv.at[q], near_r.at[q])
        for way in (RIGHT, LEFT):
            total = total + near_recv[q, way].astype(F32)
        input_grad[:, q * CHUNK : (q + 1) * CHUNK] = total.astype(BF16)

    ig_part(0)
    ig_part(1)
    ig_part(2)
    ig_far(0)
    ig_part(3)
    vw_second(False)
    ig_far(1)
    ig_far(2)
    ig_near(0)
    ig_near(1)
    ig_far(3)
    vw_second(True)
    ig_near(2)
    ig_near(3)
    ig_second(0)
    ig_second(1)
    ig_second(2)
    vw_turn()
    ig_second(3)
    left(w_raw.at[:, :, pl.ds(0, 7)], pass_s)
    left(v_send, v_s)
    left(sib, sib_s)
    left(far_send, far_s)
    ig_finish(0)
    ig_finish(1)
    ig_finish(2)
    vw_finish()
    left(line_recv.at[pl.ds(0, RING - 1)], line_s)
    ig_finish(3)
    left(near_send, near_s)


def shards(*args):
    vmem = pl.BlockSpec(memory_space=pltpu.VMEM)
    dma = pltpu.SemaphoreType.DMA
    scratch = [
        pltpu.VMEM((1, TOK), jnp.int32),
        pltpu.VMEM((TOK, 2 * HD), BF16),
        pltpu.VMEM((TOK, D), BF16),
        pltpu.VMEM((RING, 4, PAIR, TOK), BF16),
        pltpu.VMEM((CHUNKS, TOK, CHUNK), BF16),
        pltpu.VMEM((2, RING, RING, 2, ROWS, HD), BF16),
        pltpu.VMEM((4, RING, UNIT, HD), BF16),
        pltpu.VMEM((TOK, TOK), F32),
        pltpu.VMEM((TOK, 2 * HD), F32),
        pltpu.VMEM((TOK, 2 * HD), F32),
        pltpu.VMEM((TOK, 4 * HD), BF16),
        pltpu.VMEM((RING // 2, 2, RING, ROWS, HD), F32),
        pltpu.VMEM((2, 2, 7, PAIR, HD), BF16),
        pltpu.VMEM((2, 2, 7, PAIR, HD), BF16),
        pltpu.VMEM((RING, ROWS, HD), F32),
        pltpu.VMEM((RING, PADDED, HD), BF16),
        pltpu.VMEM((RING, PADDED, HD), BF16),
        pltpu.VMEM((CHUNKS, XS, 2, OWN, CHUNK), BF16),
        pltpu.VMEM((CHUNKS, XS, OWN, CHUNK), BF16),
        pltpu.VMEM((CHUNKS, OWN, CHUNK), BF16),
        pltpu.VMEM((CHUNKS, OWN, CHUNK), BF16),
        pltpu.VMEM((CHUNKS, 2, OWN, CHUNK), BF16),
        pltpu.VMEM((CHUNKS, 2, OWN, CHUNK), BF16),
        dma((5,)),
        dma(()), dma((5,)),
        dma(()), dma((2, RING)),
        dma(()), dma((2, 3, 4)), dma((2, 3, 4)), dma((2,)),
        dma(()), dma((2, 2, 2)), dma((2,)),
        dma(()), dma(()),
        dma(()), dma((2, CHUNKS)),
        dma(()), dma((CHUNKS,)),
        dma(()), dma((CHUNKS,)),
    ]
    hbm = pl.BlockSpec(memory_space=pltpu.HBM)
    return pl.pallas_call(
        kernel,
        out_shape=(jax.ShapeDtypeStruct((OWN, D), BF16), jax.ShapeDtypeStruct((ROWS, HD), F32)),
        in_specs=[hbm] * 6,
        out_specs=(vmem, vmem),
        scratch_shapes=scratch,
        compiler_params=pltpu.CompilerParams(
            collective_id=0, has_side_effects=True, vmem_limit_bytes=50 * 1024 * 1024
        ),
        name="attention_backward",
    )(*[pltpu.with_memory_space_constraint(one, pltpu.HBM) for one in args])


def solution(mesh):
    return jax.shard_map(
        shards,
        mesh=mesh,
        in_specs=(
            P(("dp", "tensor"), None),
            P("dp", None),
            P("dp", "tensor"),
            P("dp", "tensor"),
            P("dp", "tensor"),
            P("dp", "tensor"),
        ),
        out_specs=(P(("dp", "tensor"), None), P("dp", "tensor")),
        check_vma=False,
    )
```

```python
import jax
import jax.numpy as jnp
from jax import lax
from jax.experimental import pallas as pl
from jax.experimental.pallas import tpu as pltpu
from jax.sharding import PartitionSpec as P

MESH = pl.DeviceIdType.MESH
F32 = jnp.float32
BF16 = jnp.bfloat16

D = 4608
HD = 128
TOK = 256
RING = 8
XS = 4
ROWS = 72
PAIR = 2 * ROWS
UNIT = RING * ROWS
HALF = D // 2
CHUNK = 2 * UNIT
CHUNKS = D // CHUNK
OWN = 32
PADDED = 80
ENTRIES = (0, -1, 1, -2, 2, -3, 3, -4)
GROUP = 2
QUERY_SCALE = 1.0 / 12.0
MASKED = -1e30
RIGHT, LEFT = 0, 1
SIGN = (1, -1)

NT = (((1,), (1,)), ((), ()))


def dot(a, b):
    return jnp.dot(a, b, preferred_element_type=F32)


def dot_nt(a, b):
    return lax.dot_general(a, b, NT, preferred_element_type=F32)


def kernel(
    normed, seg_hbm, w_query, w_key, w_value, grad_hbm,
    input_grad, value_grad,
    seg, grad, x_buf, x_t, x_p, w_raw, w_buf, mask, q_acc, kv_acc, g_cat,
    vw, v_send, v_recv, line_sum, line_send, line_recv,
    part, sib, far_send, far_recv, near_send, near_recv,
    in_sem, x_s, x_r, first_s, first_r, pass_s, a_r, b_r, end_r,
    v_s, v_r, v_end, line_s, line_r, sib_s, sib_r, far_s, far_r, near_s, near_r,
):
    dp, tensor = lax.axis_index("dp"), lax.axis_index("tensor")
    y, z, x, core = dp // RING, dp % RING, tensor // 2, tensor % 2
    other = 1 - core

    def at(xx, yy, zz, cc):
        return (yy * RING + zz, xx * 2 + cc)

    def shift(position, by, size=RING):
        return (position + by + size) % size

    def y_dev(by):
        return at(x, shift(y, by), z, core)

    def z_dev(by):
        return at(x, y, shift(z, by), core)

    def x_dev(by):
        return at(shift(x, by, XS), y, z, core)

    sibling = at(x, y, z, other)

    def copy(src, dst, send_sem, recv_sem, device):
        return pltpu.make_async_remote_copy(
            src_ref=src, dst_ref=dst, send_sem=send_sem, recv_sem=recv_sem, device_id=device, device_id_type=MESH
        )

    def send(src, dst, send_sem, recv_sem, device):
        copy(src, dst, send_sem, recv_sem, device).start()

    def arrived(like, recv_sem):
        copy(like, like, first_s, recv_sem, sibling).wait_recv()

    def left(like, send_sem):
        copy(like, like, send_sem, line_r, sibling).wait_send()

    barrier = pltpu.get_barrier_semaphore()
    friends = [sibling, x_dev(1), x_dev(-1)]
    friends += [device(by) for device in (y_dev, z_dev) for by in (1, -1, 2, -2)]
    for friend in friends:
        pl.semaphore_signal(barrier, inc=1, device_id=friend, device_id_type=MESH)

    def rows_of(xx, cc):
        return pl.ds(pl.multiple_of((2 * xx + cc) * OWN, OWN), OWN)

    here = x_buf.at[rows_of(x, core)]
    own = [w_query.at[:, :HD], w_query.at[:, HD:], w_key, w_value]
    own_a, own_b = w_raw.at[0, y, z], w_raw.at[1, y, z]
    local = [
        pltpu.make_async_copy(src, dst, in_sem.at[i])
        for src, dst, i in (
            (own[0], own_a.at[0], 0), (own[1], own_a.at[1], 0), (own[2], own_b.at[0], 1), (own[3], own_b.at[1], 1),
            (normed, here, 2), (seg_hbm, seg, 3), (grad_hbm, grad, 4),
        )
    ]
    for one in local:
        one.start()

    pl.semaphore_wait(barrier, len(friends))

    def send_own(route, entry, device):
        for i in range(2):
            send(own[2 * route + i], w_raw.at[route, y, z, i], first_s, first_r.at[route, entry], device)

    def turn_own():
        for i in range(2):
            for way in (RIGHT, LEFT):
                by = SIGN[way]
                send(own[i], own_a.at[i], pass_s, a_r.at[way, 0, 0], y_dev(by))
                send(own[2 + i], own_b.at[i], pass_s, b_r.at[way, 0, 0], z_dev(by))

    for entry in (1, 2):
        send_own(0, entry, z_dev(-ENTRIES[entry]))
        send_own(1, entry, y_dev(-ENTRIES[entry]))
    turn_own()
    for entry in (3, 4):
        send_own(0, entry, z_dev(-ENTRIES[entry]))
        send_own(1, entry, y_dev(-ENTRIES[entry]))

    send(normed, here, x_s, x_r.at[0], x_dev(1))
    send(normed, here, x_s, x_r.at[1], x_dev(-1))
    send(normed, here, x_s, x_r.at[4], sibling)
    pltpu.make_async_copy(own_a, own_a, in_sem.at[0]).wait()
    pltpu.make_async_copy(own_b, own_b, in_sem.at[1]).wait()
    for one in local[4:]:
        one.wait()

    seg_f = seg[...].astype(F32)
    seg_col = jnp.transpose(jnp.broadcast_to(seg_f, (HD, TOK)))
    seg_col = jnp.concatenate([seg_col, seg_col], axis=1)
    key_at = lax.broadcasted_iota(jnp.int32, (TOK, TOK), 0)
    query_at = lax.broadcasted_iota(jnp.int32, (TOK, TOK), 1)
    mask[...] = jnp.where((key_at <= query_at) & (seg_col == seg_f), 1.0, 0.0).astype(F32)

    def unit_a(yy, zz):
        return w_raw.at[0, yy, zz]

    def unit_b(yy, zz):
        return w_raw.at[1, yy, zz]

    def turn(entry):
        zz, yy = shift(z, ENTRIES[entry]), shift(y, ENTRIES[entry])
        for way in (RIGHT, LEFT):
            by, slot = SIGN[way], (way, 0, entry // GROUP)
            send(unit_a(y, zz), unit_a(y, zz), pass_s, a_r.at[slot], y_dev(by))
            send(unit_b(yy, z), unit_b(yy, z), pass_s, b_r.at[slot], z_dev(by))

    def relay(way):
        by = SIGN[way]
        one, two = unit_a(y, shift(z, -2 * by)), unit_b(shift(y, -2 * by), z)
        for route, unit, device in ((0, one, z_dev), (1, two, y_dev)):
            send(unit, unit, first_s, first_r.at[route, 5 + way], device(by))
            send(unit.at[way], unit.at[way], first_s, first_r.at[route, 7], device(2 * by))

    def first_arrived(entry):
        for route in range(2):
            arrived(own_a, first_r.at[route, entry])
        if entry in (3, 4):
            relay(entry - 3)
        turn(entry)

    group_bytes = w_raw.at[0, 0, pl.ds(0, GROUP)]

    def pass_on(hop, group):
        for way in (RIGHT, LEFT):
            by = SIGN[way]
            yy, zz = shift(y, -by * hop), shift(z, -by * hop)
            entries = [GROUP * group + i for i in range(GROUP) if hop < 3 or i % 2 == way]
            arrived(group_bytes, a_r.at[way, hop - 1, group])
            for entry in entries:
                unit = unit_a(yy, shift(z, ENTRIES[entry]))
                send(unit, unit, pass_s, a_r.at[way, hop, group] if hop < 3 else end_r.at[0], y_dev(by))
            arrived(group_bytes, b_r.at[way, hop - 1, group])
            for entry in entries:
                unit = unit_b(shift(y, ENTRIES[entry]), zz)
                send(unit, unit, pass_s, b_r.at[way, hop, group] if hop < 3 else end_r.at[1], z_dev(by))

    def pass_end():
        arrived(w_raw.at[0, 0], end_r.at[0])
        arrived(w_raw.at[0, 0], end_r.at[1])

    left_half, right_half = pl.ds(0, HALF), pl.ds(HALF, HALF)
    x_right, x_left, x_far = shift(x, 1, XS), shift(x, -1, XS), shift(x, 2, XS)

    def x_block(xx, columns=None):
        rows = rows_of(xx, core)
        return x_buf.at[rows] if columns is None else x_buf.at[rows, columns]

    def x_forward():
        arrived(here, x_r.at[0])
        send(x_block(x_left, left_half), x_block(x_left, left_half), x_s, x_r.at[2], x_dev(1))
        arrived(here, x_r.at[1])
        send(x_block(x_right, right_half), x_block(x_right, right_half), x_s, x_r.at[3], x_dev(-1))
        send(x_block(x_left), x_block(x_left), x_s, x_r.at[4], sibling)
        send(x_block(x_right), x_block(x_right), x_s, x_r.at[4], sibling)

    def x_share():
        for way, columns in ((2, left_half), (3, right_half)):
            arrived(x_block(x_far, columns), x_r.at[way])
            send(x_block(x_far, columns), x_block(x_far, columns), x_s, x_r.at[4], sibling)

    def x_finish():
        arrived(x_buf.at[pl.ds(0, XS * OWN)], x_r.at[4])

    def flip(i, carry):
        columns = pl.ds(pl.multiple_of(i * CHUNK, HD), CHUNK)
        x_t[pl.ds(2 * i, 2)] = jnp.transpose(x_buf[:, columns]).reshape(2, 4, PAIR, TOK)
        return carry

    def flip_back(i, carry):
        x_p[i] = jnp.transpose(x_t[:, i].reshape(CHUNK, TOK))
        return carry

    def weights(kinds, p):
        return jnp.concatenate([w_buf[kind, pl.ds(2 * p, 2)].reshape(CHUNK, HD) for kind in kinds], axis=1)

    def q_product(p):
        both = []
        for i in range(2):
            block = w_raw[0, pl.ds(2 * p, 2), :, i].astype(F32).reshape(CHUNK, HD).astype(BF16)
            w_buf[i, pl.ds(2 * p, 2)] = block.reshape(2, UNIT, HD)
            both.append(block)
        return dot(x_buf[:, pl.ds(pl.multiple_of(p * CHUNK, HD), CHUNK)], jnp.concatenate(both, axis=1))

    def kv_product(p):
        both = []
        for i in range(2):
            block = w_raw[1, :, pl.ds(2 * p, 2), i].astype(F32).reshape(CHUNK, HD).astype(BF16)
            w_buf[2 + i, :, pl.ds(pl.multiple_of(p * PAIR, 16), PAIR), :] = block.reshape(RING, PAIR, HD)
            both.append(block)
        return dot(x_p[p], jnp.concatenate(both, axis=1))

    def order(position):
        near = 1 - 2 * ((position + 1) % 2)
        pair = position // 2
        return [pair, shift(pair, near, CHUNKS), shift(pair, -near, CHUNKS), shift(pair, 2, CHUNKS)]

    y_pairs, z_pairs = order(y), order(z)

    first_arrived(1)
    first_arrived(2)
    first_arrived(3)
    first_arrived(4)
    pass_on(1, 0)
    first_arrived(5)
    first_arrived(6)
    x_forward()
    first_arrived(7)
    pass_on(1, 1)
    pass_on(2, 0)
    pass_on(1, 2)
    pass_on(1, 3)
    pass_on(2, 1)
    pass_on(3, 0)
    x_share()
    pass_on(2, 2)
    pass_on(2, 3)
    x_finish()
    q_acc[...] = q_product(y_pairs[0])
    pass_on(3, 1)
    pass_on(3, 2)
    lax.fori_loop(0, CHUNKS, flip, 0)
    pass_on(3, 3)
    left(w_raw.at[:, 0, pl.ds(0, 7)], first_s)
    left(x_buf.at[pl.ds(0, 7 * OWN)], x_s)
    lax.fori_loop(0, CHUNKS, flip_back, 0)
    kv_acc[...] = kv_product(z_pairs[0])
    q_acc[...] += q_product(y_pairs[1])
    kv_acc[...] += kv_product(z_pairs[1])
    q_acc[...] += q_product(y_pairs[2])
    kv_acc[...] += kv_product(z_pairs[2])
    pass_end()
    kv = kv_acc[...] + kv_product(z_pairs[3])
    key, value = kv[:, :HD].astype(BF16), kv[:, HD:].astype(BF16)
    query = (q_acc[...] + q_product(y_pairs[3])).astype(BF16)

    allowed = mask[...] > 0.5
    probs, dprobs = [], []
    for h in range(2):
        scores = jnp.where(allowed, dot_nt(key, query[:, h * HD : (h + 1) * HD]) * QUERY_SCALE, MASKED)
        expo = jnp.exp(scores - jnp.max(scores, axis=0, keepdims=True))
        probs.append(expo * (1.0 / jnp.sum(expo, axis=0, keepdims=True)))
        dprobs.append(dot_nt(value, grad[:, h * HD : (h + 1) * HD]))
    rounded = [one.astype(BF16) for one in probs]
    grad_v = (dot(rounded[0], grad[:, :HD]) + dot(rounded[1], grad[:, HD:])).astype(BF16)

    for yy in range(RING):
        vw[yy // 2, yy % 2] = dot(x_t[yy].reshape(UNIT, TOK), grad_v).reshape(RING, ROWS, HD)

    def vw_y(yy, k):
        return vw[yy // 2, yy % 2, pl.ds(4 * (yy % 2) + 2 * k, 2)].reshape(PAIR, HD)

    def vw_z(zz, k):
        return vw[2 * k : 2 * k + 2, 1 - zz // 4, zz].reshape(PAIR, HD)

    routes = ((vw_y, y, y_dev), (vw_z, z, z_dev))

    def vw_send(route, way, slot, sem, device, count=1):
        one, two = [ref.at[route, way, pl.ds(slot, count)] for ref in (v_send, v_recv)]
        send(one, two, v_s, sem, device)

    def vw_first():
        for way in (RIGHT, LEFT):
            for route, (own_part, position, device) in enumerate(routes):
                by = SIGN[way]
                v_send[route, way, 2] = own_part(shift(position, 4 * by), way).astype(BF16)
                vw_send(route, way, 2, v_r.at[route, way, 1], device(2 * by))
        for way in (RIGHT, LEFT):
            for route, (own_part, position, device) in enumerate(routes):
                by = SIGN[way]
                for slot, k in ((0, 1 - way), (1, way)):
                    v_send[route, way, slot] = own_part(shift(position, 3 * by), k).astype(BF16)
                    vw_send(route, way, slot, v_r.at[route, way, slot], device(by))
        for way in (RIGHT, LEFT):
            for route, (own_part, position, device) in enumerate(routes):
                by = SIGN[way]
                for k in range(2):
                    v_send[route, way, 5 + k] = own_part(shift(position, by), k).astype(BF16)
                vw_send(route, way, 5, v_end.at[route], device(by), 2)

    def vw_second(long):
        for way in (RIGHT, LEFT):
            for route, (own_part, position, device) in enumerate(routes):
                by, k = SIGN[way], way if long else 1 - way
                total = own_part(shift(position, 2 * by), k)
                gets = (1, 2) if long else (0,)
                arrived(v_send.at[0, 0, pl.ds(0, len(gets))], v_r.at[route, way, int(long)])
                for got in gets:
                    total = total + v_recv[route, way, got].astype(F32)
                v_send[route, way, 3 + k] = total.astype(BF16)
                vw_send(route, way, 3 + k, v_end.at[route], device(2 * by))

    y_first = z // 4 == y % 2

    def vw_turn():
        for route, (own_part, position, _) in enumerate(routes):
            arrived(v_send.at[0, :, pl.ds(3, 4)], v_end.at[route])
            for k in range(2):
                total = own_part(position, k)
                for way in (RIGHT, LEFT):
                    for slot in (5 + k, 3 + k):
                        total = total + v_recv[route, way, slot].astype(F32)
                total = total.reshape(2, ROWS, HD)
                at_rows = pl.ds(4 * route + 2 * k, 2)
                line_sum[at_rows] = total
                padded = jnp.concatenate([total, jnp.zeros((2, PADDED - ROWS, HD), F32)], axis=1)
                line_send[at_rows] = padded.astype(BF16)
        for i in range(4):
            zz, yy = 4 * (y % 2) + i, 2 * i + 1 - z // 4
            one = copy(line_send.at[i], line_recv.at[z], line_s, line_r, at(x, y, zz, core))
            two = copy(line_send.at[4 + i], line_recv.at[y], line_s, line_r, at(x, yy, z, core))
            pl.when(zz != z)(one.start)
            pl.when(yy != y)(two.start)

    def vw_finish():
        arrived(line_recv.at[pl.ds(0, RING - 1)], line_r)
        position = jnp.where(y_first, z, y)
        total = line_sum[jnp.where(y_first, z % 4, 4 + y // 2)]
        for by in range(1, RING):
            total = total + line_recv[shift(position, by)].astype(F32)[:ROWS]
        value_grad[...] = total * float(TOK * RING * RING) ** (-0.5)

    vw_first()

    dscores = []
    for h in range(2):
        delta = jnp.sum(rounded[h].astype(F32) * dprobs[h], axis=0, keepdims=True)
        dscores.append((probs[h] * (dprobs[h] - delta) * QUERY_SCALE).astype(BF16))
    key_t = jnp.transpose(key)
    for h in range(2):
        g_cat[:, h * HD : (h + 1) * HD] = jnp.transpose(dot(key_t, dscores[h])).astype(BF16)
    g_cat[:, 2 * HD : 3 * HD] = (dot(dscores[0], query[:, :HD]) + dot(dscores[1], query[:, HD:])).astype(BF16)
    g_cat[:, 3 * HD :] = grad_v

    def ig_part(q):
        both = dot_nt(g_cat[...], weights((0, 1, 2, 3), q)).astype(BF16)
        part[q] = both.reshape(XS, 2, OWN, CHUNK)
        for xx, sem in ((x_far, 0), (x_right, 1), (x_left, 1), (x, 1)):
            send(part.at[q, xx, other], sib.at[q, xx], sib_s, sib_r.at[sem, q], sibling)

    def chip_sum(q, xx):
        return part[q, xx, core].astype(F32) + sib[q, xx].astype(F32)

    def near(q, way):
        send(near_send.at[q, way], near_recv.at[q, way], near_s, near_r.at[q], x_dev(SIGN[way]))

    def ig_far(q):
        arrived(sib.at[q, 0], sib_r.at[0, q])
        far_send[q] = chip_sum(q, x_far).astype(BF16)
        send(far_send.at[q], far_recv.at[q], far_s, far_r.at[q], x_dev(SIGN[q % 2]))

    def ig_near(q):
        way = 1 - q % 2
        arrived(sib.at[q, pl.ds(0, 3)], sib_r.at[1, q])
        near_send[q, way] = chip_sum(q, shift(x, SIGN[way], XS)).astype(BF16)
        near(q, way)

    def ig_second(q):
        way = q % 2
        arrived(far_recv.at[q], far_r.at[q])
        near_send[q, way] = (chip_sum(q, shift(x, SIGN[way], XS)) + far_recv[q].astype(F32)).astype(BF16)
        near(q, way)

    def ig_finish(q):
        total = chip_sum(q, x)
        arrived(near_recv.at[q], near_r.at[q])
        for way in (RIGHT, LEFT):
            total = total + near_recv[q, way].astype(F32)
        input_grad[:, q * CHUNK : (q + 1) * CHUNK] = total.astype(BF16)

    ig_part(0)
    ig_part(1)
    ig_part(2)
    ig_far(0)
    ig_part(3)
    vw_second(False)
    ig_far(1)
    ig_far(2)
    ig_near(0)
    ig_near(1)
    ig_far(3)
    vw_second(True)
    ig_near(2)
    ig_near(3)
    ig_second(0)
    ig_second(1)
    ig_second(2)
    vw_turn()
    ig_second(3)
    left(w_raw.at[:, :, pl.ds(0, 7)], pass_s)
    left(v_send, v_s)
    left(sib, sib_s)
    left(far_send, far_s)
    ig_finish(0)
    ig_finish(1)
    ig_finish(2)
    vw_finish()
    left(line_recv.at[pl.ds(0, RING - 1)], line_s)
    ig_finish(3)
    left(near_send, near_s)


def store(input_grad, value_grad, input_grad_out, value_grad_out, sems):
    copies = [
        pltpu.make_async_copy(input_grad, input_grad_out, sems.at[0]),
        pltpu.make_async_copy(value_grad, value_grad_out, sems.at[1]),
    ]
    for one in copies:
        one.start()
    for one in copies:
        one.wait()


def shards(*args):
    vmem = pl.BlockSpec(memory_space=pltpu.VMEM)
    dma = pltpu.SemaphoreType.DMA
    scratch = [
        pltpu.VMEM((1, TOK), jnp.int32),
        pltpu.VMEM((TOK, 2 * HD), BF16),
        pltpu.VMEM((TOK, D), BF16),
        pltpu.VMEM((RING, 4, PAIR, TOK), BF16),
        pltpu.VMEM((CHUNKS, TOK, CHUNK), BF16),
        pltpu.VMEM((2, RING, RING, 2, ROWS, HD), BF16),
        pltpu.VMEM((4, RING, UNIT, HD), BF16),
        pltpu.VMEM((TOK, TOK), F32),
        pltpu.VMEM((TOK, 2 * HD), F32),
        pltpu.VMEM((TOK, 2 * HD), F32),
        pltpu.VMEM((TOK, 4 * HD), BF16),
        pltpu.VMEM((RING // 2, 2, RING, ROWS, HD), F32),
        pltpu.VMEM((2, 2, 7, PAIR, HD), BF16),
        pltpu.VMEM((2, 2, 7, PAIR, HD), BF16),
        pltpu.VMEM((RING, ROWS, HD), F32),
        pltpu.VMEM((RING, PADDED, HD), BF16),
        pltpu.VMEM((RING, PADDED, HD), BF16),
        pltpu.VMEM((CHUNKS, XS, 2, OWN, CHUNK), BF16),
        pltpu.VMEM((CHUNKS, XS, OWN, CHUNK), BF16),
        pltpu.VMEM((CHUNKS, OWN, CHUNK), BF16),
        pltpu.VMEM((CHUNKS, OWN, CHUNK), BF16),
        pltpu.VMEM((CHUNKS, 2, OWN, CHUNK), BF16),
        pltpu.VMEM((CHUNKS, 2, OWN, CHUNK), BF16),
        dma((5,)),
        dma(()), dma((5,)),
        dma(()), dma((2, RING)),
        dma(()), dma((2, 3, 4)), dma((2, 3, 4)), dma((2,)),
        dma(()), dma((2, 2, 2)), dma((2,)),
        dma(()), dma(()),
        dma(()), dma((2, CHUNKS)),
        dma(()), dma((CHUNKS,)),
        dma(()), dma((CHUNKS,)),
    ]
    hbm = pl.BlockSpec(memory_space=pltpu.HBM)
    results = pl.pallas_call(
        kernel,
        out_shape=(jax.ShapeDtypeStruct((OWN, D), BF16), jax.ShapeDtypeStruct((ROWS, HD), F32)),
        in_specs=[hbm] * 6,
        out_specs=(vmem, vmem),
        scratch_shapes=scratch,
        compiler_params=pltpu.CompilerParams(
            collective_id=0, has_side_effects=True, vmem_limit_bytes=50 * 1024 * 1024
        ),
        name="attention_backward",
    )(*[pltpu.with_memory_space_constraint(one, pltpu.HBM) for one in args])
    return pl.pallas_call(
        store,
        out_shape=(jax.ShapeDtypeStruct((OWN, D), BF16), jax.ShapeDtypeStruct((ROWS, HD), F32)),
        in_specs=[vmem] * 2,
        out_specs=(hbm, hbm),
        scratch_shapes=[dma((2,))],
        compiler_params=pltpu.CompilerParams(vmem_limit_bytes=4 * 1024 * 1024),
        name="store",
    )(*results)


def solution(mesh):
    return jax.shard_map(
        shards,
        mesh=mesh,
        in_specs=(
            P(("dp", "tensor"), None),
            P("dp", None),
            P("dp", "tensor"),
            P("dp", "tensor"),
            P("dp", "tensor"),
            P("dp", "tensor"),
        ),
        out_specs=(P(("dp", "tensor"), None), P("dp", "tensor")),
        check_vma=False,
    )
```

```python
import jax
import jax.numpy as jnp
from jax import lax
from jax.experimental import pallas as pl
from jax.experimental.pallas import tpu as pltpu
from jax.sharding import PartitionSpec as P

MESH = pl.DeviceIdType.MESH
F32 = jnp.float32
BF16 = jnp.bfloat16

D = 4608
HD = 128
TOK = 256
RING = 8
XS = 4
ROWS = 72
PAIR = 2 * ROWS
UNIT = RING * ROWS
HALF = D // 2
CHUNK = 2 * UNIT
CHUNKS = D // CHUNK
OWN = 32
PADDED = 80
ENTRIES = (0, -1, 1, -2, 2, -3, 3, -4)
GROUP = 2
QUERY_SCALE = 1.0 / 12.0
MASKED = -1e30
RIGHT, LEFT = 0, 1
SIGN = (1, -1)

NT = (((1,), (1,)), ((), ()))


def dot(a, b):
    return jnp.dot(a, b, preferred_element_type=F32)


def dot_nt(a, b):
    return lax.dot_general(a, b, NT, preferred_element_type=F32)


def kernel(
    normed, seg_hbm, w_query, w_key, w_value, grad_hbm,
    input_grad, value_grad,
    seg, grad, x_buf, x_t, x_p, w_raw, w_buf, mask, q_acc, kv_acc, g_cat,
    vw, v_send, v_recv, line_sum, line_send, line_recv,
    part, sib, far_send, far_recv, near_send, near_recv,
    in_sem, x_s, x_r, first_s, first_r, pass_s, a_r, b_r, end_r,
    v_s, v_r, v_end, line_s, line_r, sib_s, sib_r, far_s, far_r, near_s, near_r,
):
    dp, tensor = lax.axis_index("dp"), lax.axis_index("tensor")
    y, z, x, core = dp // RING, dp % RING, tensor // 2, tensor % 2
    other = 1 - core

    def at(xx, yy, zz, cc):
        return (yy * RING + zz, xx * 2 + cc)

    def shift(position, by, size=RING):
        return (position + by + size) % size

    def y_dev(by):
        return at(x, shift(y, by), z, core)

    def z_dev(by):
        return at(x, y, shift(z, by), core)

    def x_dev(by):
        return at(shift(x, by, XS), y, z, core)

    sibling = at(x, y, z, other)

    def copy(src, dst, send_sem, recv_sem, device):
        return pltpu.make_async_remote_copy(
            src_ref=src, dst_ref=dst, send_sem=send_sem, recv_sem=recv_sem, device_id=device, device_id_type=MESH
        )

    def send(src, dst, send_sem, recv_sem, device):
        copy(src, dst, send_sem, recv_sem, device).start()

    def arrived(like, recv_sem):
        copy(like, like, first_s, recv_sem, sibling).wait_recv()

    def left(like, send_sem):
        copy(like, like, send_sem, line_r, sibling).wait_send()

    barrier = pltpu.get_barrier_semaphore()
    friends = [sibling, x_dev(1), x_dev(-1)]
    friends += [device(by) for device in (y_dev, z_dev) for by in (1, -1, 2, -2)]
    for friend in friends:
        pl.semaphore_signal(barrier, inc=1, device_id=friend, device_id_type=MESH)

    def rows_of(xx, cc):
        return pl.ds(pl.multiple_of((2 * xx + cc) * OWN, OWN), OWN)

    here = x_buf.at[rows_of(x, core)]
    own = [w_query.at[:, :HD], w_query.at[:, HD:], w_key, w_value]
    own_a, own_b = w_raw.at[0, y, z], w_raw.at[1, y, z]
    local = [
        pltpu.make_async_copy(src, dst, in_sem.at[i])
        for src, dst, i in (
            (own[0], own_a.at[0], 0), (own[1], own_a.at[1], 0), (own[2], own_b.at[0], 1), (own[3], own_b.at[1], 1),
            (normed, here, 2), (seg_hbm, seg, 3), (grad_hbm, grad, 4),
        )
    ]
    for one in local:
        one.start()

    pl.semaphore_wait(barrier, len(friends))

    def unit_a(yy, zz):
        return w_raw.at[0, yy, zz]

    def unit_b(yy, zz):
        return w_raw.at[1, yy, zz]

    def turn(entry):
        zz, yy = shift(z, ENTRIES[entry]), shift(y, ENTRIES[entry])
        for way in (RIGHT, LEFT):
            by, slot = SIGN[way], (way, 0, entry // GROUP)
            send(unit_a(y, zz), unit_a(y, zz), pass_s, a_r.at[slot], y_dev(by))
            send(unit_b(yy, z), unit_b(yy, z), pass_s, b_r.at[slot], z_dev(by))

    def relay(way):
        by = SIGN[way]
        one, two = unit_a(y, shift(z, -2 * by)), unit_b(shift(y, -2 * by), z)
        for route, unit, device in ((0, one, z_dev), (1, two, y_dev)):
            send(unit, unit, first_s, first_r.at[route, 5 + way], device(by))
            send(unit.at[way], unit.at[way], first_s, first_r.at[route, 7], device(2 * by))

    def first_arrived(entry):
        for route in range(2):
            arrived(own_a, first_r.at[route, entry])
        if entry in (3, 4):
            relay(entry - 3)
        turn(entry)

    def send_own(entry):
        send(own_a, own_a, first_s, first_r.at[0, entry], z_dev(-ENTRIES[entry]))
        send(own_b, own_b, first_s, first_r.at[1, entry], y_dev(-ENTRIES[entry]))

    pltpu.make_async_copy(own_a, own_a, in_sem.at[0]).wait()
    pltpu.make_async_copy(own_b, own_b, in_sem.at[1]).wait()
    send_own(1)
    send_own(2)
    turn(0)
    send_own(3)
    send_own(4)
    send(normed, here, x_s, x_r.at[0], x_dev(1))
    send(normed, here, x_s, x_r.at[1], x_dev(-1))
    send(normed, here, x_s, x_r.at[4], sibling)
    for one in local[4:]:
        one.wait()

    seg_f = seg[...].astype(F32)
    seg_col = jnp.transpose(jnp.broadcast_to(seg_f, (HD, TOK)))
    seg_col = jnp.concatenate([seg_col, seg_col], axis=1)
    key_at = lax.broadcasted_iota(jnp.int32, (TOK, TOK), 0)
    query_at = lax.broadcasted_iota(jnp.int32, (TOK, TOK), 1)
    mask[...] = jnp.where((key_at <= query_at) & (seg_col == seg_f), 1.0, 0.0).astype(F32)

    group_bytes = w_raw.at[0, 0, pl.ds(0, GROUP)]

    def pass_on(hop, group):
        for way in (RIGHT, LEFT):
            by = SIGN[way]
            yy, zz = shift(y, -by * hop), shift(z, -by * hop)
            entries = [GROUP * group + i for i in range(GROUP) if hop < 3 or i % 2 == way]
            arrived(group_bytes, a_r.at[way, hop - 1, group])
            for entry in entries:
                unit = unit_a(yy, shift(z, ENTRIES[entry]))
                send(unit, unit, pass_s, a_r.at[way, hop, group] if hop < 3 else end_r.at[0], y_dev(by))
            arrived(group_bytes, b_r.at[way, hop - 1, group])
            for entry in entries:
                unit = unit_b(shift(y, ENTRIES[entry]), zz)
                send(unit, unit, pass_s, b_r.at[way, hop, group] if hop < 3 else end_r.at[1], z_dev(by))

    def pass_end():
        arrived(w_raw.at[0, 0], end_r.at[0])
        arrived(w_raw.at[0, 0], end_r.at[1])

    left_half, right_half = pl.ds(0, HALF), pl.ds(HALF, HALF)
    x_right, x_left, x_far = shift(x, 1, XS), shift(x, -1, XS), shift(x, 2, XS)

    def x_block(xx, columns=None):
        rows = rows_of(xx, core)
        return x_buf.at[rows] if columns is None else x_buf.at[rows, columns]

    def x_forward():
        arrived(here, x_r.at[0])
        send(x_block(x_left, left_half), x_block(x_left, left_half), x_s, x_r.at[2], x_dev(1))
        arrived(here, x_r.at[1])
        send(x_block(x_right, right_half), x_block(x_right, right_half), x_s, x_r.at[3], x_dev(-1))
        send(x_block(x_left), x_block(x_left), x_s, x_r.at[4], sibling)
        send(x_block(x_right), x_block(x_right), x_s, x_r.at[4], sibling)

    def x_share():
        for way, columns in ((2, left_half), (3, right_half)):
            arrived(x_block(x_far, columns), x_r.at[way])
            send(x_block(x_far, columns), x_block(x_far, columns), x_s, x_r.at[4], sibling)

    def x_finish():
        arrived(x_buf.at[pl.ds(0, XS * OWN)], x_r.at[4])

    def flip(i, carry):
        columns = pl.ds(pl.multiple_of(i * CHUNK, HD), CHUNK)
        x_t[pl.ds(2 * i, 2)] = jnp.transpose(x_buf[:, columns]).reshape(2, 4, PAIR, TOK)
        return carry

    def flip_back(i, carry):
        x_p[i] = jnp.transpose(x_t[:, i].reshape(CHUNK, TOK))
        return carry

    def weights(kinds, p):
        return jnp.concatenate([w_buf[kind, pl.ds(2 * p, 2)].reshape(CHUNK, HD) for kind in kinds], axis=1)

    def q_product(p):
        both = []
        for i in range(2):
            block = w_raw[0, pl.ds(2 * p, 2), :, i].astype(F32).reshape(CHUNK, HD).astype(BF16)
            w_buf[i, pl.ds(2 * p, 2)] = block.reshape(2, UNIT, HD)
            both.append(block)
        return dot(x_buf[:, pl.ds(pl.multiple_of(p * CHUNK, HD), CHUNK)], jnp.concatenate(both, axis=1))

    def kv_product(p):
        both = []
        for i in range(2):
            block = w_raw[1, :, pl.ds(2 * p, 2), i].astype(F32).reshape(CHUNK, HD).astype(BF16)
            w_buf[2 + i, :, pl.ds(pl.multiple_of(p * PAIR, 16), PAIR), :] = block.reshape(RING, PAIR, HD)
            both.append(block)
        return dot(x_p[p], jnp.concatenate(both, axis=1))

    def order(position):
        near = 1 - 2 * ((position + 1) % 2)
        pair = position // 2
        return [pair, shift(pair, near, CHUNKS), shift(pair, -near, CHUNKS), shift(pair, 2, CHUNKS)]

    y_pairs, z_pairs = order(y), order(z)

    first_arrived(1)
    first_arrived(2)
    first_arrived(3)
    first_arrived(4)
    pass_on(1, 0)
    first_arrived(5)
    first_arrived(6)
    x_forward()
    first_arrived(7)
    pass_on(1, 1)
    pass_on(2, 0)
    pass_on(1, 2)
    pass_on(1, 3)
    pass_on(2, 1)
    pass_on(3, 0)
    x_share()
    pass_on(2, 2)
    pass_on(2, 3)
    x_finish()
    q_acc[...] = q_product(y_pairs[0])
    pass_on(3, 1)
    pass_on(3, 2)
    lax.fori_loop(0, CHUNKS, flip, 0)
    pass_on(3, 3)
    left(w_raw.at[:, 0, pl.ds(0, 7)], first_s)
    left(x_buf.at[pl.ds(0, 7 * OWN)], x_s)
    lax.fori_loop(0, CHUNKS, flip_back, 0)
    kv_acc[...] = kv_product(z_pairs[0])
    q_acc[...] += q_product(y_pairs[1])
    kv_acc[...] += kv_product(z_pairs[1])
    q_acc[...] += q_product(y_pairs[2])
    kv_acc[...] += kv_product(z_pairs[2])
    pass_end()
    kv = kv_acc[...] + kv_product(z_pairs[3])
    key, value = kv[:, :HD].astype(BF16), kv[:, HD:].astype(BF16)
    query = (q_acc[...] + q_product(y_pairs[3])).astype(BF16)

    allowed = mask[...] > 0.5
    probs, dprobs = [], []
    for h in range(2):
        scores = jnp.where(allowed, dot_nt(key, query[:, h * HD : (h + 1) * HD]) * QUERY_SCALE, MASKED)
        expo = jnp.exp(scores - jnp.max(scores, axis=0, keepdims=True))
        probs.append(expo * (1.0 / jnp.sum(expo, axis=0, keepdims=True)))
        dprobs.append(dot_nt(value, grad[:, h * HD : (h + 1) * HD]))
    rounded = [one.astype(BF16) for one in probs]
    grad_v = (dot(rounded[0], grad[:, :HD]) + dot(rounded[1], grad[:, HD:])).astype(BF16)

    for yy in range(RING):
        vw[yy // 2, yy % 2] = dot(x_t[yy].reshape(UNIT, TOK), grad_v).reshape(RING // 2, 2, ROWS, HD)

    def vw_y(yy, k):
        return vw[yy // 2, yy % 2, 2 * k : 2 * k + 2, yy % 2].reshape(PAIR, HD)

    def vw_z(zz, k):
        return vw[2 * k : 2 * k + 2, 1 - zz % 2, zz // 2, zz % 2].reshape(PAIR, HD)

    routes = ((vw_y, y, y_dev), (vw_z, z, z_dev))

    def vw_send(route, way, slot, sem, device, count=1):
        one, two = [ref.at[route, way, pl.ds(slot, count)] for ref in (v_send, v_recv)]
        send(one, two, v_s, sem, device)

    def vw_first():
        for way in (RIGHT, LEFT):
            for route, (own_part, position, device) in enumerate(routes):
                by = SIGN[way]
                v_send[route, way, 2] = own_part(shift(position, 4 * by), way).astype(BF16)
                vw_send(route, way, 2, v_r.at[route, way, 1], device(2 * by))
        for way in (RIGHT, LEFT):
            for route, (own_part, position, device) in enumerate(routes):
                by = SIGN[way]
                for slot, k in ((0, 1 - way), (1, way)):
                    v_send[route, way, slot] = own_part(shift(position, 3 * by), k).astype(BF16)
                    vw_send(route, way, slot, v_r.at[route, way, slot], device(by))
        for way in (RIGHT, LEFT):
            for route, (own_part, position, device) in enumerate(routes):
                by = SIGN[way]
                for k in range(2):
                    v_send[route, way, 5 + k] = own_part(shift(position, by), k).astype(BF16)
                vw_send(route, way, 5, v_end.at[route], device(by), 2)

    def vw_second(long):
        for way in (RIGHT, LEFT):
            for route, (own_part, position, device) in enumerate(routes):
                by, k = SIGN[way], way if long else 1 - way
                total = own_part(shift(position, 2 * by), k)
                gets = (1, 2) if long else (0,)
                arrived(v_send.at[0, 0, pl.ds(0, len(gets))], v_r.at[route, way, int(long)])
                for got in gets:
                    total = total + v_recv[route, way, got].astype(F32)
                v_send[route, way, 3 + k] = total.astype(BF16)
                vw_send(route, way, 3 + k, v_end.at[route], device(2 * by))

    y_first = z % 2 == y % 2

    def vw_turn():
        for route, (own_part, position, _) in enumerate(routes):
            arrived(v_send.at[0, :, pl.ds(3, 4)], v_end.at[route])
            for k in range(2):
                total = own_part(position, k)
                for way in (RIGHT, LEFT):
                    for slot in (5 + k, 3 + k):
                        total = total + v_recv[route, way, slot].astype(F32)
                total = total.reshape(2, ROWS, HD)
                at_rows = pl.ds(4 * route + 2 * k, 2)
                line_sum[at_rows] = total
                padded = jnp.concatenate([total, jnp.zeros((2, PADDED - ROWS, HD), F32)], axis=1)
                line_send[at_rows] = padded.astype(BF16)
        for i in range(4):
            zz, yy = 2 * i + y % 2, 2 * i + 1 - z % 2
            one = copy(line_send.at[i], line_recv.at[z], line_s, line_r, at(x, y, zz, core))
            two = copy(line_send.at[4 + i], line_recv.at[y], line_s, line_r, at(x, yy, z, core))
            pl.when(zz != z)(one.start)
            pl.when(yy != y)(two.start)

    def vw_finish():
        arrived(line_recv.at[pl.ds(0, RING - 1)], line_r)
        position = jnp.where(y_first, z, y)
        total = line_sum[jnp.where(y_first, z // 2, 4 + y // 2)]
        for by in range(1, RING):
            total = total + line_recv[shift(position, by)].astype(F32)[:ROWS]
        value_grad[...] = total * float(TOK * RING * RING) ** (-0.5)

    vw_first()

    dscores = []
    for h in range(2):
        delta = jnp.sum(rounded[h].astype(F32) * dprobs[h], axis=0, keepdims=True)
        dscores.append((probs[h] * (dprobs[h] - delta) * QUERY_SCALE).astype(BF16))
    key_t = jnp.transpose(key)
    for h in range(2):
        g_cat[:, h * HD : (h + 1) * HD] = jnp.transpose(dot(key_t, dscores[h])).astype(BF16)
    g_cat[:, 2 * HD : 3 * HD] = (dot(dscores[0], query[:, :HD]) + dot(dscores[1], query[:, HD:])).astype(BF16)
    g_cat[:, 3 * HD :] = grad_v

    def ig_part(q):
        both = dot_nt(g_cat[...], weights((0, 1, 2, 3), q)).astype(BF16)
        part[q] = both.reshape(XS, 2, OWN, CHUNK)
        for xx, sem in ((x_far, 0), (x_right, 1), (x_left, 1), (x, 1)):
            send(part.at[q, xx, other], sib.at[q, xx], sib_s, sib_r.at[sem, q], sibling)

    def chip_sum(q, xx):
        return part[q, xx, core].astype(F32) + sib[q, xx].astype(F32)

    def near(q, way):
        send(near_send.at[q, way], near_recv.at[q, way], near_s, near_r.at[q], x_dev(SIGN[way]))

    def ig_far(q):
        arrived(sib.at[q, 0], sib_r.at[0, q])
        far_send[q] = chip_sum(q, x_far).astype(BF16)
        send(far_send.at[q], far_recv.at[q], far_s, far_r.at[q], x_dev(SIGN[q % 2]))

    def ig_near(q):
        way = 1 - q % 2
        arrived(sib.at[q, pl.ds(0, 3)], sib_r.at[1, q])
        near_send[q, way] = chip_sum(q, shift(x, SIGN[way], XS)).astype(BF16)
        near(q, way)

    def ig_second(q):
        way = q % 2
        arrived(far_recv.at[q], far_r.at[q])
        near_send[q, way] = (chip_sum(q, shift(x, SIGN[way], XS)) + far_recv[q].astype(F32)).astype(BF16)
        near(q, way)

    def ig_finish(q):
        total = chip_sum(q, x)
        arrived(near_recv.at[q], near_r.at[q])
        for way in (RIGHT, LEFT):
            total = total + near_recv[q, way].astype(F32)
        input_grad[:, q * CHUNK : (q + 1) * CHUNK] = total.astype(BF16)

    ig_part(0)
    ig_part(1)
    ig_part(2)
    ig_far(0)
    ig_part(3)
    ig_far(1)
    vw_second(False)
    ig_far(2)
    ig_far(3)
    ig_near(0)
    ig_near(1)
    vw_second(True)
    ig_near(2)
    ig_near(3)
    ig_second(0)
    ig_second(1)
    ig_second(2)
    vw_turn()
    ig_second(3)
    left(w_raw.at[:, :, pl.ds(0, 7)], pass_s)
    left(v_send, v_s)
    left(sib, sib_s)
    left(far_send, far_s)
    ig_finish(0)
    ig_finish(1)
    ig_finish(2)
    vw_finish()
    left(line_recv.at[pl.ds(0, RING - 1)], line_s)
    ig_finish(3)
    left(near_send, near_s)


def store(input_grad, value_grad, input_grad_out, value_grad_out, sems):
    copies = [
        pltpu.make_async_copy(input_grad, input_grad_out, sems.at[0]),
        pltpu.make_async_copy(value_grad, value_grad_out, sems.at[1]),
    ]
    for one in copies:
        one.start()
    for one in copies:
        one.wait()


def shards(*args):
    vmem = pl.BlockSpec(memory_space=pltpu.VMEM)
    dma = pltpu.SemaphoreType.DMA
    scratch = [
        pltpu.VMEM((1, TOK), jnp.int32),
        pltpu.VMEM((TOK, 2 * HD), BF16),
        pltpu.VMEM((TOK, D), BF16),
        pltpu.VMEM((RING, 4, PAIR, TOK), BF16),
        pltpu.VMEM((CHUNKS, TOK, CHUNK), BF16),
        pltpu.VMEM((2, RING, RING, 2, ROWS, HD), BF16),
        pltpu.VMEM((4, RING, UNIT, HD), BF16),
        pltpu.VMEM((TOK, TOK), F32),
        pltpu.VMEM((TOK, 2 * HD), F32),
        pltpu.VMEM((TOK, 2 * HD), F32),
        pltpu.VMEM((TOK, 4 * HD), BF16),
        pltpu.VMEM((RING // 2, 2, RING // 2, 2, ROWS, HD), F32),
        pltpu.VMEM((2, 2, 7, PAIR, HD), BF16),
        pltpu.VMEM((2, 2, 7, PAIR, HD), BF16),
        pltpu.VMEM((RING, ROWS, HD), F32),
        pltpu.VMEM((RING, PADDED, HD), BF16),
        pltpu.VMEM((RING, PADDED, HD), BF16),
        pltpu.VMEM((CHUNKS, XS, 2, OWN, CHUNK), BF16),
        pltpu.VMEM((CHUNKS, XS, OWN, CHUNK), BF16),
        pltpu.VMEM((CHUNKS, OWN, CHUNK), BF16),
        pltpu.VMEM((CHUNKS, OWN, CHUNK), BF16),
        pltpu.VMEM((CHUNKS, 2, OWN, CHUNK), BF16),
        pltpu.VMEM((CHUNKS, 2, OWN, CHUNK), BF16),
        dma((5,)),
        dma(()), dma((5,)),
        dma(()), dma((2, RING)),
        dma(()), dma((2, 3, 4)), dma((2, 3, 4)), dma((2,)),
        dma(()), dma((2, 2, 2)), dma((2,)),
        dma(()), dma(()),
        dma(()), dma((2, CHUNKS)),
        dma(()), dma((CHUNKS,)),
        dma(()), dma((CHUNKS,)),
    ]
    hbm = pl.BlockSpec(memory_space=pltpu.HBM)
    results = pl.pallas_call(
        kernel,
        out_shape=(jax.ShapeDtypeStruct((OWN, D), BF16), jax.ShapeDtypeStruct((ROWS, HD), F32)),
        in_specs=[hbm] * 6,
        out_specs=(vmem, vmem),
        scratch_shapes=scratch,
        compiler_params=pltpu.CompilerParams(
            collective_id=0, has_side_effects=True, vmem_limit_bytes=50 * 1024 * 1024
        ),
        name="attention_backward",
    )(*[pltpu.with_memory_space_constraint(one, pltpu.HBM) for one in args])
    return pl.pallas_call(
        store,
        out_shape=(jax.ShapeDtypeStruct((OWN, D), BF16), jax.ShapeDtypeStruct((ROWS, HD), F32)),
        in_specs=[vmem] * 2,
        out_specs=(hbm, hbm),
        scratch_shapes=[dma((2,))],
        compiler_params=pltpu.CompilerParams(vmem_limit_bytes=4 * 1024 * 1024),
        name="store",
    )(*results)


def solution(mesh):
    return jax.shard_map(
        shards,
        mesh=mesh,
        in_specs=(
            P(("dp", "tensor"), None),
            P("dp", None),
            P("dp", "tensor"),
            P("dp", "tensor"),
            P("dp", "tensor"),
            P("dp", "tensor"),
        ),
        out_specs=(P(("dp", "tensor"), None), P("dp", "tensor")),
        check_vma=False,
    )
```
